32 devices in a mesh: gx: 4 (over y, core), gy: 8 (over z, x).
Axes of the slice: x: 2, y: 2, z: 4, core: 2. Of those that a mesh axis runs over, the one named last changes fastest.
Arguments:
- owned_surplus: float32 [4096, 16, 256], P(('gx', 'gy')), may hold values from -0.6 to 0.6
- tile_owner: int32 [4096], replicated, may hold values from 0 to 31, as said below
- grid_levels: int32 [8, 2], replicated, may hold values from 0 to 3, as said below
- coefficients: int32 [8], replicated, may hold values from 1 to 3
- faulty_grids: int32 [2], replicated, may hold values from 1 to 7
- velocity_x: float32 [2048, 8192], P('gx', 'gy'), may hold values from -1 to 1
- velocity_y: float32 [2048, 8192], P('gx', 'gy'), may hold values from -1 to 1
Outputs:
- solution: float32 [2048, 8192], P('gx', 'gy')
The draws below stay inside these ranges and needn't reach their ends.
Inputs may be any that keep to these rules, and one draw needn't show every extreme that they name: tile_owner[d * 128 + k] = (d + o_k) mod (the number of devices), with offsets o_k that depend only on k; no offset value serves more than 8 of the 128 values of k, and some offset value serves exactly 8. `grid_levels`: row 0 is (0, 0), the full grid.
All inputs are finite; a program needn't handle non-finite values.
Results may differ from the reference program's by a relative error of at most 0.00011.
Values sent between devices are 32-bit elements; how exact they have to be, the bound alone decides.
A program may use at most 128 MiB of HBM per device.

```python
import jax
import jax.numpy as jnp
import numpy as np
from jax import lax

CX = 512
CY = 1024
TILE_ROWS = 32
TILE_COLS = 4
GRIDS = 8
FAULTS = 2
STEPS = 2
SLOTS = 128
TX = 16
TY = 256
NX = 2048
NY = 8192
DEVICES = 32


def draw_tile_owner(key, part):
    device_total = NX // CX * (NY // CY)
    capacity = 2 * SLOTS // device_total
    quarter = device_total // 4
    counts_list = [capacity] * quarter + [capacity // 2] * (2 * quarter) + [0] * (device_total - 3 * quarter)
    rank_of_slot = np.repeat(np.arange(device_total), np.array(counts_list))
    order_values = jax.random.permutation(jax.random.fold_in(key, 11), device_total)
    offsets = order_values[jnp.asarray(rank_of_slot, dtype=jnp.int32)]
    offsets = jax.random.permutation(jax.random.fold_in(key, 12), offsets)
    dest_ids = jnp.arange(device_total, dtype=jnp.int32)[:, None]
    return ((dest_ids + offsets[None, :]) % device_total).reshape(-1).astype(jnp.int32)


def draw_grid_levels(key, part):
    drops = jax.random.randint(jax.random.fold_in(key, 21), (GRIDS, 2), 0, 4)
    drops = drops.at[0].set(0)
    drops = drops.at[1, 0].set(3)
    return drops.astype(jnp.int32)


def with_ends(values, stream_key, low, high):
    spot = [jax.random.randint(jax.random.fold_in(stream_key, axis), (), 0, length) for axis, length in enumerate(values.shape)]
    longest = values.shape.index(max(values.shape))
    neighbour = spot[:longest] + [(spot[longest] + 1) % values.shape[longest]] + spot[longest + 1:]
    return values.at[tuple(spot)].set(low).at[tuple(neighbour)].set(high)


def block_levels(rng, shape, pieces, least, high):
    gain = 1.0
    for position, blocks in pieces:
        steps = jax.random.uniform(jax.random.fold_in(jax.random.fold_in(rng, 6), position), (blocks,), jnp.float32, least / len(pieces), high / len(pieces))
        gain = gain * jnp.repeat(jnp.exp(steps), shape[position] // blocks).reshape((-1,) + (1,) * (len(shape) - 1 - position))
    return gain


def normal_values(stream_key, shape, width, reach, cuts=(), kind=jnp.bfloat16):
    level = block_levels(stream_key, shape, cuts, -0.22, 0.18) if cuts else 1.0
    values = jax.random.normal(stream_key, shape, jnp.float32) * width * level
    return jnp.minimum(jnp.maximum(values, -reach), reach).astype(kind)


def setup_inputs(seed: int = 0) -> dict:
    keys = jax.random.split(jax.random.key(seed), 8)
    return {
        "owned_surplus": normal_values(keys[0], (DEVICES * SLOTS, TX, TY), 0.1, 0.6, ((0, 32),), jnp.float32),
        "tile_owner": draw_tile_owner(jax.random.fold_in(keys[7], 71), 0),
        "grid_levels": draw_grid_levels(jax.random.fold_in(keys[7], 71), 0),
        "coefficients": with_ends(jax.random.randint(keys[3], (GRIDS,), 1, 4), jax.random.fold_in(keys[3], 1), 1, 3).astype(jnp.int32),
        "faulty_grids": jax.random.randint(keys[4], (FAULTS,), 1, GRIDS).astype(jnp.int32),
        "velocity_x": jnp.clip(jax.random.uniform(keys[5], (NX, NY), jnp.float32, -1.0, 1.0) * block_levels(keys[5], (NX, NY), ((0, 4), (1, 8)), -0.4, 0.0), -1.0, 1.0),
        "velocity_y": jnp.clip(jax.random.uniform(keys[6], (NX, NY), jnp.float32, -1.0, 1.0) * block_levels(keys[6], (NX, NY), ((0, 4), (1, 8)), -0.4, 0.0), -1.0, 1.0),
    }


TIME_STEP = 0.2
DIFFUSION = 0.5


def level_of(index_row, top_level):
    result = jnp.full(index_row.shape, top_level, jnp.int32)
    for bit_pos in range(1, top_level + 1):
        result = jnp.where(index_row % (2 ** bit_pos) == 0, top_level - bit_pos, result)
    return result


def weight_table(grid_levels, coefficients, faulty_grids, top_x, top_y):
    grid_count = coefficients.shape[0]
    grid_ids = jnp.arange(grid_count, dtype=jnp.int32)
    alive_mask = jnp.all(faulty_grids[None, :] != grid_ids[:, None], axis=1)
    grid_share = jnp.where(alive_mask, coefficients, 0).astype(jnp.float32)
    covers_x = (jnp.arange(top_x + 1, dtype=jnp.int32)[:, None] <= (top_x - grid_levels[None, :, 0])).astype(jnp.float32)
    covers_y = (jnp.arange(top_y + 1, dtype=jnp.int32)[:, None] <= (top_y - grid_levels[None, :, 1])).astype(jnp.float32)
    return jnp.dot(covers_x * grid_share[None, :], covers_y.T, precision=lax.Precision.HIGHEST)


def refine(values, ends_next):
    spacing = values.shape[0] // 2
    while spacing >= 1:
        corners = jnp.concatenate([values[0::2 * spacing], ends_next], axis=0)
        middle = values[spacing::2 * spacing]
        values = values.at[spacing::2 * spacing].set(middle + 0.5 * (corners[:-1] + corners[1:]))
        spacing = spacing // 2
    return values


def rates(padded, vel_x, vel_y):
    centre = padded[2:-2, 2:-2]
    east_one = padded[3:-1, 2:-2]
    west_one = padded[1:-3, 2:-2]
    east_two = padded[4:, 2:-2]
    west_two = padded[:-4, 2:-2]
    north_one = padded[2:-2, 3:-1]
    south_one = padded[2:-2, 1:-3]
    north_two = padded[2:-2, 4:]
    south_two = padded[2:-2, :-4]
    slope_x = (8.0 * (east_one - west_one) - (east_two - west_two)) / 12.0
    slope_y = (8.0 * (north_one - south_one) - (north_two - south_two)) / 12.0
    curve_x = (16.0 * (east_one + west_one) - (east_two + west_two) - 30.0 * centre) / 12.0
    curve_y = (16.0 * (north_one + south_one) - (north_two + south_two) - 30.0 * centre) / 12.0
    return DIFFUSION * (curve_x + curve_y) - vel_x * slope_x - vel_y * slope_y


def reference(owned_surplus, tile_owner, grid_levels, coefficients, faulty_grids, velocity_x, velocity_y):
    tile_index = jnp.arange(tile_owner.shape[0], dtype=jnp.int32)
    source_rows = (tile_owner * SLOTS + tile_index % SLOTS).astype(jnp.int32)
    tile_data = jnp.take(owned_surplus, source_rows, axis=0)
    blocks_x = NX // CX
    blocks_y = NY // CY
    grid = tile_data.reshape(blocks_x, blocks_y, TILE_ROWS, TILE_COLS, TX, TY)
    grid = grid.transpose(0, 2, 4, 1, 3, 5).reshape(NX, NY)
    top_x = int(NX).bit_length() - 1
    top_y = int(NY).bit_length() - 1
    table = weight_table(grid_levels, coefficients, faulty_grids, top_x, top_y)
    levels_x = level_of(jnp.arange(NX, dtype=jnp.int32), top_x)
    levels_y = level_of(jnp.arange(NY, dtype=jnp.int32), top_y)
    weights = jnp.take(jnp.take(table, levels_x, axis=0), levels_y, axis=1)
    surplus = grid * weights
    nodal_x = refine(surplus, surplus[0:1])
    flipped = nodal_x.T
    nodal = refine(flipped, flipped[0:1]).T
    field_now = nodal
    for step_index in range(STEPS):
        first_rate = rates(jnp.pad(field_now, 2, mode="wrap"), velocity_x, velocity_y)
        middle_field = field_now + TIME_STEP * first_rate
        second_rate = rates(jnp.pad(middle_field, 2, mode="wrap"), velocity_x, velocity_y)
        field_now = 0.5 * (field_now + middle_field + TIME_STEP * second_rate)
    return field_now
```

```python
import functools

import jax
import jax.numpy as jnp
import ml_dtypes
import numpy as np
from jax import lax
from jax.experimental import pallas as pl
from jax.experimental.pallas import tpu as pltpu
from jax.sharding import PartitionSpec as P

STEPS = 2
TIME_STEP = 0.2
CHUNK = 256
HALO = 8
TOP = 16
MESH = pl.DeviceIdType.MESH


def hat_matrix():
    points = np.arange(CHUNK)[:, None]
    nodes = np.arange(CHUNK)[None, :]
    reach = np.where(nodes == 0, 1, nodes & -nodes)
    hats = np.maximum(0.0, 1.0 - np.abs(points - nodes) / reach)
    hats[:, 0] = 0.0
    return hats


def coarse_matrix(count):
    values = np.eye(count)
    spacing = count // 2
    while spacing >= 1:
        for x in range(spacing, count, 2 * spacing):
            values[x] += 0.5 * (values[x - spacing] + values[(x + spacing) % count])
        spacing //= 2
    return values


def coarse_rows(size, per_device):
    full = coarse_matrix(size * per_device)
    table = np.zeros((size, 8, size * 8))
    for me in range(size):
        for row in range(per_device + 1):
            point = (me * per_device + row) % (size * per_device)
            for j in range(size * per_device):
                table[me, row, (j // per_device) * 8 + j % per_device] = full[point, j]
    return table.astype(np.float32)


def split_dot(matrix, values, left):
    high = values.astype(jnp.bfloat16)
    low = (values - high.astype(jnp.float32)).astype(jnp.bfloat16)
    if left:
        return jnp.dot(matrix, high, preferred_element_type=jnp.float32) + jnp.dot(
            matrix, low, preferred_element_type=jnp.float32
        )
    return jnp.dot(high, matrix, preferred_element_type=jnp.float32) + jnp.dot(
        low, matrix, preferred_element_type=jnp.float32
    )


def exact_dot(a, b):
    return jnp.dot(a, b, precision=lax.Precision.HIGHEST, preferred_element_type=jnp.float32)


def kernel(
    size_x,
    size_y,
    place_ref,
    weight_ref,
    incoming_ref,
    vel_x_ref,
    vel_y_ref,
    hats_ref,
    hats_t_ref,
    coarse_x_ref,
    coarse_y_ref,
    out_ref,
    block,
    fields,
    middle,
    rows_all,
    cols_all,
    col_send,
    col_recv,
    local_sem,
    rows_send_sem,
    rows_recv_sem,
    cols_send_sem,
    cols_recv_sem,
    face_send_sem,
    face_recv_sem,
    side_send_sem,
    side_recv_sem,
):
    rows, cols = out_ref.shape
    tile_rows, tile_cols = weight_ref.shape
    across = cols // tile_cols
    ix = lax.axis_index("gx")
    iy = lax.axis_index("gy")

    loads = [
        pltpu.make_async_copy(
            source, fields.at[f, pl.ds(TOP, rows), pl.ds(0, cols)], local_sem.at[f]
        )
        for f, source in ((1, vel_x_ref), (2, vel_y_ref))
    ]
    for load in loads:
        load.start()

    barrier = pltpu.get_barrier_semaphore()
    for step in range(1, size_x):
        pl.semaphore_signal(
            barrier, inc=1, device_id=(lax.rem(ix + step, size_x), iy), device_id_type=MESH
        )
    for step in range(1, size_y):
        pl.semaphore_signal(
            barrier, inc=1, device_id=(ix, lax.rem(iy + step, size_y)), device_id_type=MESH
        )
    pl.semaphore_wait(barrier, size_x + size_y - 2)

    before_x = (lax.rem(ix + size_x - 1, size_x), iy)
    after_x = (lax.rem(ix + 1, size_x), iy)
    before_y = (ix, lax.rem(iy + size_y - 1, size_y))
    after_y = (ix, lax.rem(iy + 1, size_y))

    def faces(f):
        return [
            pltpu.make_async_remote_copy(
                src_ref=fields.at[f, pl.ds(start, HALO), pl.ds(0, cols)],
                dst_ref=fields.at[f, pl.ds(target, HALO), pl.ds(0, cols)],
                send_sem=face_send_sem.at[f, side],
                recv_sem=face_recv_sem.at[f, side],
                device_id=device,
                device_id_type=MESH,
            )
            for side, start, target, device in (
                (0, TOP, TOP + rows, before_x),
                (1, TOP + rows - HALO, TOP - HALO, after_x),
            )
        ]

    def sides(f):
        col_send[f, 0] = fields[f, :, 0:128].T[0:HALO]
        col_send[f, 1] = fields[f, :, cols - 128 : cols].T[128 - HALO : 128]
        return [
            pltpu.make_async_remote_copy(
                src_ref=col_send.at[f, side],
                dst_ref=col_recv.at[f, side],
                send_sem=side_send_sem.at[f, side],
                recv_sem=side_recv_sem.at[f, side],
                device_id=device,
                device_id_type=MESH,
            )
            for side, device in ((0, before_y), (1, after_y))
        ]

    def fill_sides(f):
        length = col_recv.shape[3]
        strip = jnp.concatenate(
            [
                col_recv[f, 0],
                jnp.zeros((128 - 2 * HALO, length), jnp.float32),
                col_recv[f, 1],
            ],
            axis=0,
        )
        fields[f, :, cols : cols + 128] = strip.T

    for load in loads:
        load.wait()
    vel_faces = faces(1) + faces(2)
    for copy in vel_faces:
        copy.start()

    weight = weight_ref[...]

    def put(kx, carry):
        for ky in range(across):
            start = pl.multiple_of(kx * tile_rows, tile_rows)
            block[pl.ds(start, tile_rows), ky * tile_cols : (ky + 1) * tile_cols] = (
                incoming_ref[place_ref[kx * across + ky]] * weight
            )
        return carry

    lax.fori_loop(0, rows // tile_rows, put, 0)

    chunks_x = rows // CHUNK
    chunks_y = cols // CHUNK
    rows_all[ix] = jnp.concatenate(
        [block[c * CHUNK : c * CHUNK + 1, :] for c in range(chunks_x)]
        + [jnp.zeros((8 - chunks_x, cols), jnp.float32)],
        axis=0,
    )
    row_copies = [
        pltpu.make_async_remote_copy(
            src_ref=rows_all.at[ix],
            dst_ref=rows_all.at[ix],
            send_sem=rows_send_sem.at[step],
            recv_sem=rows_recv_sem.at[step],
            device_id=(lax.rem(ix + step, size_x), iy),
            device_id_type=MESH,
        )
        for step in range(1, size_x)
    ]
    for copy in row_copies:
        copy.start()

    for copy in vel_faces:
        copy.wait()
    vel_sides = sides(1) + sides(2)
    for copy in vel_sides:
        copy.start()

    for copy in row_copies:
        copy.wait()
    corners = exact_dot(coarse_x_ref[ix], rows_all[...].reshape(size_x * 8, cols))
    part = lax.broadcasted_iota(jnp.int32, (CHUNK, 1), 0).astype(jnp.float32) * (1.0 / CHUNK)
    for c in range(chunks_x):
        inner = split_dot(hats_ref[...], block[c * CHUNK : (c + 1) * CHUNK, :], True)
        block[c * CHUNK : (c + 1) * CHUNK, :] = (
            inner + (1.0 - part) * corners[c : c + 1] + part * corners[c + 1 : c + 2]
        )

    lane = lax.broadcasted_iota(jnp.int32, (rows, 128), 1)
    picked = jnp.zeros((rows, 128), jnp.float32)
    for c in range(chunks_y):
        column = block[:, c * CHUNK : c * CHUNK + 1]
        picked = jnp.where(lane == c, column, picked)
    cols_all[iy] = picked.T[0:8]
    col_copies = [
        pltpu.make_async_remote_copy(
            src_ref=cols_all.at[iy],
            dst_ref=cols_all.at[iy],
            send_sem=cols_send_sem.at[step],
            recv_sem=cols_recv_sem.at[step],
            device_id=(ix, lax.rem(iy + step, size_y)),
            device_id_type=MESH,
        )
        for step in range(1, size_y)
    ]
    for copy in col_copies:
        copy.start()

    for c in range(chunks_y):
        span = slice(c * CHUNK, (c + 1) * CHUNK)
        block[:, span] = split_dot(hats_t_ref[...], block[:, span], False)

    for copy in vel_sides:
        copy.wait()
    fill_sides(1)
    fill_sides(2)

    for copy in col_copies:
        copy.wait()
    corners = exact_dot(coarse_y_ref[iy], cols_all[...].reshape(size_y * 8, rows))
    corners = jnp.concatenate([corners, jnp.zeros((120, rows), jnp.float32)], axis=0).T
    part = lax.broadcasted_iota(jnp.int32, (1, CHUNK), 1).astype(jnp.float32) * (1.0 / CHUNK)
    for c in range(chunks_y):
        span = slice(c * CHUNK, (c + 1) * CHUNK)
        fields[0, TOP : TOP + rows, span] = (
            block[:, span]
            + (1.0 - part) * corners[:, c : c + 1]
            + part * corners[:, c + 1 : c + 2]
        )

    own_faces = faces(0)
    for copy in own_faces:
        copy.start()
    for copy in own_faces:
        copy.wait()
    own_sides = sides(0)
    for copy in own_sides:
        copy.start()
    for copy in own_sides:
        copy.wait()
    fill_sides(0)

    width = cols + 128
    scale = TIME_STEP / 12.0

    def change(read, start):
        centre = read(start, 0)
        west_one, east_one = read(start, -1), read(start, 1)
        west_two, east_two = read(start, -2), read(start, 2)
        north_one = pltpu.roll(centre, width - 1, 1)
        south_one = pltpu.roll(centre, 1, 1)
        north_two = pltpu.roll(centre, width - 2, 1)
        south_two = pltpu.roll(centre, 2, 1)
        near = (east_one + west_one) + (north_one + south_one)
        far = (east_two + west_two) + (north_two + south_two)
        slope_x = 8.0 * (east_one - west_one) - (east_two - west_two)
        slope_y = 8.0 * (north_one - south_one) - (north_two - south_two)
        vel_x = fields[1, pl.ds(start, 8), :]
        vel_y = fields[2, pl.ds(start, 8), :]
        total = (8.0 * near - 0.5 * far - 30.0 * centre) - vel_x * slope_x - vel_y * slope_y
        return centre, scale * total

    def read_field(start, shift):
        around = fields.at[0, pl.ds(pl.multiple_of(start - 8, 8), 24), :]
        return around[8 + shift : 16 + shift, :]

    def read_middle(start, shift):
        around = middle.at[pl.ds(pl.multiple_of(start - 8, 8), 24), :]
        return around[8 + shift : 16 + shift, :]

    for step in range(STEPS):
        last = step == STEPS - 1

        def first_half(i, carry):
            start = pl.multiple_of(i * 8, 8)
            centre, delta = change(read_field, start)
            middle[pl.ds(start, 8), :] = centre + delta
            return carry

        lax.fori_loop(TOP // 8 - 1, (TOP + rows) // 8 + 1, first_half, 0)

        def second_half(i, carry):
            start = pl.multiple_of(i * 8, 8)
            centre, delta = change(read_middle, start)
            value = 0.5 * (fields[0, pl.ds(start, 8), :] + centre + delta)
            if last:
                out_ref[pl.ds(pl.multiple_of(start - TOP, 8), 8), :] = value[:, :cols]
            else:
                fields[0, pl.ds(start, 8), :] = value
            return carry

        edge = 0 if last else 1
        lax.fori_loop(TOP // 8 - edge, (TOP + rows) // 8 + edge, second_half, 0)


def restart(place, weight, incoming, vel_x, vel_y, size_x, size_y):
    rows, cols = vel_x.shape
    frame = (rows + 2 * TOP + 127) // 128 * 128
    hats = hat_matrix()
    operands = (
        place,
        weight,
        incoming,
        vel_x,
        vel_y,
        jnp.asarray(hats.astype(ml_dtypes.bfloat16)),
        jnp.asarray(hats.T.astype(ml_dtypes.bfloat16)),
        jnp.asarray(coarse_rows(size_x, rows // CHUNK)),
        jnp.asarray(coarse_rows(size_y, cols // CHUNK)),
    )
    vmem = pl.BlockSpec(memory_space=pltpu.VMEM)
    hbm = pl.BlockSpec(memory_space=pl.ANY)
    dma = pltpu.SemaphoreType.DMA
    return pl.pallas_call(
        functools.partial(kernel, size_x, size_y),
        out_shape=jax.ShapeDtypeStruct((rows, cols), jnp.float32),
        in_specs=[pl.BlockSpec(memory_space=pltpu.SMEM), vmem, vmem, hbm, hbm] + [vmem] * 4,
        out_specs=vmem,
        scratch_shapes=[
            pltpu.VMEM((rows, cols), jnp.float32),
            pltpu.VMEM((3, frame, cols + 128), jnp.float32),
            pltpu.VMEM((frame, cols + 128), jnp.float32),
            pltpu.VMEM((size_x, 8, cols), jnp.float32),
            pltpu.VMEM((size_y, 8, rows), jnp.float32),
            pltpu.VMEM((3, 2, HALO, frame), jnp.float32),
            pltpu.VMEM((3, 2, HALO, frame), jnp.float32),
            dma((3,)),
            dma((size_x,)),
            dma((size_x,)),
            dma((size_y,)),
            dma((size_y,)),
            dma((3, 2)),
            dma((3, 2)),
            dma((3, 2)),
            dma((3, 2)),
        ],
        compiler_params=pltpu.CompilerParams(
            collective_id=0, has_side_effects=True, vmem_limit_bytes=50 * 2**20
        ),
        name="restart",
    )(*operands)


def tile_weights(grid_levels, coefficients, faulty_grids, shape):
    grid_ids = jnp.arange(coefficients.shape[0], dtype=jnp.int32)
    alive = jnp.all(faulty_grids[None, :] != grid_ids[:, None], axis=1)
    share = jnp.where(alive, coefficients, 0).astype(jnp.float32)
    masks = jnp.left_shift(1, grid_levels) - 1
    row = jnp.arange(shape[0], dtype=jnp.int32)
    col = jnp.arange(shape[1], dtype=jnp.int32)
    on_row = (row[None, :] & masks[:, 0:1]) == 0
    on_col = (col[None, :] & masks[:, 1:2]) == 0
    return jnp.sum(
        jnp.where(on_row[:, :, None] & on_col[:, None, :], share[:, None, None], 0.0), axis=0
    )


def local(
    owned_surplus, tile_owner, grid_levels, coefficients, faulty_grids, velocity_x, velocity_y
):
    slot_count, tile_height, tile_width = owned_surplus.shape
    size_x = lax.axis_size("gx")
    size_y = lax.axis_size("gy")
    device_count = size_x * size_y
    capacity = 2 * slot_count // device_count
    own_index = lax.axis_index("gx") * size_y + lax.axis_index("gy")
    offsets = tile_owner[:slot_count]
    positions = jnp.arange(slot_count, dtype=jnp.int32)
    same_offset = offsets[:, None] == offsets[None, :]
    earlier = positions[None, :] < positions[:, None]
    slot_rank = jnp.sum((same_offset & earlier).astype(jnp.int32), axis=1)
    target = (own_index - offsets) % device_count
    seat = target * capacity + slot_rank
    seats = jnp.arange(device_count * capacity, dtype=jnp.int32)
    holder = jnp.max(jnp.where(seat[None, :] == seats[:, None], positions[None, :], 0), axis=1)
    outgoing = jnp.take(owned_surplus, holder, axis=0, mode="clip")
    incoming = lax.all_to_all(
        outgoing.reshape(device_count, capacity, tile_height, tile_width),
        ("gx", "gy"),
        split_axis=0,
        concat_axis=0,
        tiled=True,
    )
    incoming = incoming.reshape(device_count * capacity, tile_height, tile_width)
    place = (own_index + offsets) % device_count * capacity + slot_rank
    weight = tile_weights(grid_levels, coefficients, faulty_grids, (tile_height, tile_width))
    return restart(place, weight, incoming, velocity_x, velocity_y, size_x, size_y)


def solution(mesh):
    return jax.shard_map(
        local,
        mesh=mesh,
        in_specs=(P(("gx", "gy"), None, None), P(), P(), P(), P(), P("gx", "gy"), P("gx", "gy")),
        out_specs=P("gx", "gy"),
        check_vma=False,
    )
```

```python
import functools

import jax
import jax.numpy as jnp
import ml_dtypes
import numpy as np
from jax import lax
from jax.experimental import pallas as pl
from jax.experimental.pallas import tpu as pltpu
from jax.sharding import PartitionSpec as P

STEPS = 2
TIME_STEP = 0.2
CHUNK = 256
HALO = 8
TOP = 16
MESH = pl.DeviceIdType.MESH


def hat_matrix():
    points = np.arange(CHUNK)[:, None]
    nodes = np.arange(CHUNK)[None, :]
    reach = np.where(nodes == 0, 1, nodes & -nodes)
    hats = np.maximum(0.0, 1.0 - np.abs(points - nodes) / reach)
    hats[:, 0] = 0.0
    return hats


def coarse_matrix(count):
    values = np.eye(count)
    spacing = count // 2
    while spacing >= 1:
        for x in range(spacing, count, 2 * spacing):
            values[x] += 0.5 * (values[x - spacing] + values[(x + spacing) % count])
        spacing //= 2
    return values


FIRST = tuple(range(1, 9)) + (16, 32, 64, 128)
LAST = (128, 192, 224, 240) + tuple(range(248, 256))
PACK = 16


def frame_table(size, per_device, length, corner_row, right_row, left_row):
    total = size * per_device
    full = coarse_matrix(total)
    hats = hat_matrix()
    table = np.zeros((size, length, size * 8 + 2 * PACK))
    spots = np.array([(j // per_device) * 8 + j % per_device for j in range(total)])
    for me in range(size):
        for c in range(per_device + 1):
            table[me, corner_row + c, spots] = full[(me * per_device + c) % total]
        for k in range(HALO):
            for row, chunk, point, nodes, start in (
                (right_row + k, (me + 1) * per_device, k, FIRST, size * 8),
                (left_row + k, me * per_device - 1, CHUNK - HALO + k, LAST, size * 8 + PACK),
            ):
                part = point / CHUNK
                table[me, row, spots] = (1 - part) * full[chunk % total] + part * full[
                    (chunk + 1) % total
                ]
                for i, node in enumerate(nodes):
                    table[me, row, start + i] = hats[point, node]
    return table.astype(np.float32)


def split_dot(matrix, values, left):
    high = values.astype(jnp.bfloat16)
    low = (values - high.astype(jnp.float32)).astype(jnp.bfloat16)
    if left:
        return jnp.dot(matrix, high, preferred_element_type=jnp.float32) + jnp.dot(
            matrix, low, preferred_element_type=jnp.float32
        )
    return jnp.dot(high, matrix, preferred_element_type=jnp.float32) + jnp.dot(
        low, matrix, preferred_element_type=jnp.float32
    )


def exact_dot(a, b):
    return jnp.dot(a, b, precision=lax.Precision.HIGHEST, preferred_element_type=jnp.float32)


def kernel(
    size_x,
    size_y,
    place_ref,
    weight_ref,
    outgoing_ref,
    vel_x_ref,
    vel_y_ref,
    hats_ref,
    hats_t_ref,
    table_x_ref,
    table_y_ref,
    out_ref,
    incoming,
    block,
    field,
    middle,
    later,
    vel_x,
    vel_y,
    rows_all,
    row_send,
    row_recv,
    cols_all,
    col_send,
    col_recv,
    side_send,
    side_recv,
    local_sem,
    tile_send_sem,
    tile_recv_sem,
    rows_sem,
    row_pack_sem,
    cols_sem,
    col_pack_sem,
    face_sem,
    side_sem,
):
    rows, cols = out_ref.shape
    tile_rows, tile_cols = weight_ref.shape
    across = cols // tile_cols
    devices = size_x * size_y
    capacity = incoming.shape[0] // devices
    frame = block.shape[0]
    chunks_x = rows // CHUNK
    chunks_y = cols // CHUNK
    ix = lax.axis_index("gx")
    iy = lax.axis_index("gy")
    me = ix * size_y + iy
    before_x = (lax.rem(ix + size_x - 1, size_x), iy)
    after_x = (lax.rem(ix + 1, size_x), iy)
    before_y = (ix, lax.rem(iy + size_y - 1, size_y))
    after_y = (ix, lax.rem(iy + 1, size_y))

    def remote(src, dst, send_sem, recv_sem, device):
        return pltpu.make_async_remote_copy(
            src_ref=src,
            dst_ref=dst,
            send_sem=send_sem,
            recv_sem=recv_sem,
            device_id=device,
            device_id_type=MESH,
        )

    def partner(step):
        other = lax.rem(me + step, devices)
        return (other // size_y, lax.rem(other, size_y))

    own_tiles = pl.ds(pl.multiple_of(me * capacity, capacity), capacity)
    loads = [
        pltpu.make_async_copy(
            source, target.at[pl.ds(TOP, rows), pl.ds(0, cols)], local_sem.at[f]
        )
        for f, source, target in ((0, vel_x_ref, vel_x), (1, vel_y_ref, vel_y))
    ]
    loads.append(
        pltpu.make_async_copy(outgoing_ref.at[own_tiles], incoming.at[own_tiles], local_sem.at[2])
    )
    for load in loads:
        load.start()

    barrier = pltpu.get_barrier_semaphore()

    def greet(step, carry):
        pl.semaphore_signal(barrier, inc=1, device_id=partner(step), device_id_type=MESH)
        return carry

    lax.fori_loop(1, devices, greet, 0)
    pl.semaphore_wait(barrier, devices - 1)

    def tile_copy(step):
        other = lax.rem(me + step, devices)
        return remote(
            outgoing_ref.at[pl.ds(pl.multiple_of(other * capacity, capacity), capacity)],
            incoming.at[own_tiles],
            tile_send_sem.at[step],
            tile_recv_sem.at[step],
            partner(step),
        )

    for load in loads[:2]:
        load.wait()
    face_copies = [
        remote(
            vel.at[pl.ds(start, HALO), pl.ds(0, cols)],
            vel.at[pl.ds(target, HALO), pl.ds(0, cols)],
            face_sem.at[f, side, 0],
            face_sem.at[f, side, 1],
            device,
        )
        for f, vel in enumerate((vel_x, vel_y))
        for side, start, target, device in (
            (0, TOP, TOP + rows, before_x),
            (1, TOP + rows - HALO, TOP - HALO, after_x),
        )
    ]
    for copy in face_copies:
        copy.start()

    def send_tiles(step, carry):
        tile_copy(step).start()
        return carry

    lax.fori_loop(1, devices, send_tiles, 0)

    for copy in face_copies:
        copy.wait()
    side_copies = []
    for f, vel in enumerate((vel_x, vel_y)):
        side_send[f, 0] = vel[:, 0:128].T[0:HALO]
        side_send[f, 1] = vel[:, cols - 128 : cols].T[128 - HALO : 128]
        for side, device in ((0, before_y), (1, after_y)):
            side_copies.append(
                remote(
                    side_send.at[f, side],
                    side_recv.at[f, side],
                    side_sem.at[f, side, 0],
                    side_sem.at[f, side, 1],
                    device,
                )
            )
    for copy in side_copies:
        copy.start()
    for copy in side_copies:
        copy.wait()
    for f, vel in enumerate((vel_x, vel_y)):
        strip = jnp.concatenate(
            [
                side_recv[f, 0],
                jnp.zeros((128 - 2 * HALO, frame), jnp.float32),
                side_recv[f, 1],
            ],
            axis=0,
        )
        vel[:, cols : cols + 128] = strip.T

    loads[2].wait()

    def receive_tiles(step, carry):
        tile_copy(step).wait()
        return carry

    lax.fori_loop(1, devices, receive_tiles, 0)

    weight = weight_ref[...]

    def put(kx, carry):
        start = pl.multiple_of(TOP + kx * tile_rows, tile_rows)
        for ky in range(across):
            block[pl.ds(start, tile_rows), ky * tile_cols : (ky + 1) * tile_cols] = (
                incoming[place_ref[kx * across + ky]] * weight
            )
        return carry

    lax.fori_loop(0, rows // tile_rows, put, 0, unroll=2)

    def row(point):
        return block[TOP + point : TOP + point + 1, :]

    def pack_rows(start, nodes):
        return jnp.concatenate(
            [row(start + node) for node in nodes]
            + [jnp.zeros((PACK - len(nodes), cols), jnp.float32)],
            axis=0,
        )

    rows_all[ix] = jnp.concatenate(
        [row(c * CHUNK) for c in range(chunks_x)]
        + [jnp.zeros((8 - chunks_x, cols), jnp.float32)],
        axis=0,
    )
    row_send[0] = pack_rows(0, FIRST)
    row_send[1] = pack_rows(rows - CHUNK, LAST)
    row_copies = [
        remote(
            rows_all.at[ix],
            rows_all.at[ix],
            rows_sem.at[step, 0],
            rows_sem.at[step, 1],
            (lax.rem(ix + step, size_x), iy),
        )
        for step in range(1, size_x)
    ] + [
        remote(
            row_send.at[side],
            row_recv.at[side],
            row_pack_sem.at[side, 0],
            row_pack_sem.at[side, 1],
            device,
        )
        for side, device in ((0, before_x), (1, after_x))
    ]
    for copy in row_copies:
        copy.start()

    for c in range(chunks_x):
        span = slice(TOP + c * CHUNK, TOP + (c + 1) * CHUNK)
        block[span, :] = split_dot(hats_ref[...], block[span, :], True)

    for copy in row_copies:
        copy.wait()
    known = jnp.concatenate(
        [rows_all[...].reshape(size_x * 8, cols), row_recv[...].reshape(2 * PACK, cols)], axis=0
    )
    ends = exact_dot(table_x_ref[ix], known)
    part = lax.broadcasted_iota(jnp.int32, (CHUNK, 1), 0).astype(jnp.float32) * (1.0 / CHUNK)
    for c in range(chunks_x):
        span = slice(TOP + c * CHUNK, TOP + (c + 1) * CHUNK)
        block[span, :] += (1.0 - part) * ends[c : c + 1] + part * ends[c + 1 : c + 2]
    block[TOP + rows : TOP + rows + HALO, :] = ends[8:16]
    block[TOP - HALO : TOP, :] = ends[16:24]

    lane = lax.broadcasted_iota(jnp.int32, (frame, 128), 1)
    picked = block[:, 0:128]
    for spot, point in enumerate([128] + [c * CHUNK for c in range(1, chunks_y)]):
        picked = jnp.where(lane == 10 + spot, block[:, point : point + 1], picked)
    first = picked.T
    last_cols = block[:, cols - 128 : cols].T
    blank = jnp.zeros((8, frame), jnp.float32)
    cols_all[iy] = jnp.concatenate(
        [first[0:1], first[11 : 10 + chunks_y], blank[: 8 - chunks_y]], axis=0
    )
    col_send[0] = jnp.concatenate(
        [first[1:9], first[16:17], first[32:33], first[64:65], first[10:11], blank[:4]], axis=0
    )
    col_send[1] = jnp.concatenate(
        [last_cols[node - 128 : node - 127] for node in LAST] + [blank[:4]], axis=0
    )
    col_copies = [
        remote(
            cols_all.at[iy],
            cols_all.at[iy],
            cols_sem.at[step, 0],
            cols_sem.at[step, 1],
            (ix, lax.rem(iy + step, size_y)),
        )
        for step in range(1, size_y)
    ] + [
        remote(
            col_send.at[side],
            col_recv.at[side],
            col_pack_sem.at[side, 0],
            col_pack_sem.at[side, 1],
            device,
        )
        for side, device in ((0, before_y), (1, after_y))
    ]
    for copy in col_copies:
        copy.start()

    used = rows + 2 * TOP
    for c in range(chunks_y):
        span = slice(c * CHUNK, (c + 1) * CHUNK)
        block[0:used, span] = split_dot(hats_t_ref[...], block[0:used, span], False)

    for copy in col_copies:
        copy.wait()
    known = jnp.concatenate(
        [cols_all[...].reshape(size_y * 8, frame), col_recv[...].reshape(2 * PACK, frame)], axis=0
    )
    ends = exact_dot(table_y_ref[iy], known).T
    field[:, cols : cols + 128] = ends
    part = lax.broadcasted_iota(jnp.int32, (1, CHUNK), 1).astype(jnp.float32) * (1.0 / CHUNK)
    for c in range(chunks_y):
        span = slice(c * CHUNK, (c + 1) * CHUNK)
        field[0:used, span] = (
            block[0:used, span]
            + (1.0 - part) * ends[0:used, 8 + c : 9 + c]
            + part * ends[0:used, 9 + c : 10 + c]
        )

    width = cols + 128
    scale = TIME_STEP / 12.0

    def change(ref, start):
        around = ref.at[pl.ds(pl.multiple_of(start - 8, 8), 24), :]

        def read(shift):
            return around[8 + shift : 16 + shift, :]

        centre = read(0)
        west_one, east_one = read(-1), read(1)
        west_two, east_two = read(-2), read(2)
        north_one = pltpu.roll(centre, width - 1, 1)
        south_one = pltpu.roll(centre, 1, 1)
        north_two = pltpu.roll(centre, width - 2, 1)
        south_two = pltpu.roll(centre, 2, 1)
        near = (east_one + west_one) + (north_one + south_one)
        far = (east_two + west_two) + (north_two + south_two)
        slope_x = 8.0 * (east_one - west_one) - (east_two - west_two)
        slope_y = 8.0 * (north_one - south_one) - (north_two - south_two)
        total = (8.0 * near - 0.5 * far - 30.0 * centre) - (
            vel_x[pl.ds(start, 8), :] * slope_x + vel_y[pl.ds(start, 8), :] * slope_y
        )
        return centre, scale * total

    def sweep(start, count, body):
        def strip(i, carry):
            body(pl.multiple_of(start + i * 8, 8))
            return carry

        group = next(g for g in (8, 6, 4, 3, 2, 1) if count % g == 0)
        lax.fori_loop(0, count, strip, 0, unroll=group)

    now, then = field, later
    for step in range(STEPS):
        last = step == STEPS - 1

        def first_half(start, now=now):
            centre, delta = change(now, start)
            middle[pl.ds(start, 8), :] = centre + delta

        def second_half(start, now=now, then=then, last=last):
            centre, delta = change(middle, start)
            value = 0.5 * (now[pl.ds(start, 8), :] + centre + delta)
            if last:
                out_ref[pl.ds(pl.multiple_of(start - TOP, 8), 8), :] = value[:, :cols]
            else:
                then[pl.ds(start, 8), :] = value

        sweep(TOP - HALO, (rows + 2 * HALO) // 8, first_half)
        if last:
            sweep(TOP, rows // 8, second_half)
        else:
            sweep(TOP - HALO, (rows + 2 * HALO) // 8, second_half)
        now, then = then, now


def restart(place, weight, outgoing, vel_x, vel_y, size_x, size_y):
    rows, cols = vel_x.shape
    frame = (rows + 2 * TOP + 127) // 128 * 128
    devices = size_x * size_y
    hats = hat_matrix()
    operands = (
        place,
        weight,
        outgoing,
        vel_x,
        vel_y,
        jnp.asarray(hats.astype(ml_dtypes.bfloat16)),
        jnp.asarray(hats.T.astype(ml_dtypes.bfloat16)),
        jnp.asarray(frame_table(size_x, rows // CHUNK, 24, 0, 8, 16)),
        jnp.asarray(frame_table(size_y, cols // CHUNK, 128, 8, 0, 120)),
    )
    vmem = pl.BlockSpec(memory_space=pltpu.VMEM)
    hbm = pl.BlockSpec(memory_space=pl.ANY)
    dma = pltpu.SemaphoreType.DMA
    framed = pltpu.VMEM((frame, cols + 128), jnp.float32)
    return pl.pallas_call(
        functools.partial(kernel, size_x, size_y),
        out_shape=jax.ShapeDtypeStruct((rows, cols), jnp.float32),
        in_specs=[pl.BlockSpec(memory_space=pltpu.SMEM), vmem, hbm, hbm, hbm] + [vmem] * 4,
        out_specs=vmem,
        scratch_shapes=[
            pltpu.VMEM(outgoing.shape, jnp.float32),
            pltpu.VMEM((frame, cols), jnp.float32),
            framed,
            framed,
            framed,
            framed,
            framed,
            pltpu.VMEM((size_x, 8, cols), jnp.float32),
            pltpu.VMEM((2, PACK, cols), jnp.float32),
            pltpu.VMEM((2, PACK, cols), jnp.float32),
            pltpu.VMEM((size_y, 8, frame), jnp.float32),
            pltpu.VMEM((2, PACK, frame), jnp.float32),
            pltpu.VMEM((2, PACK, frame), jnp.float32),
            pltpu.VMEM((2, 2, HALO, frame), jnp.float32),
            pltpu.VMEM((2, 2, HALO, frame), jnp.float32),
            dma((3,)),
            dma((devices,)),
            dma((devices,)),
            dma((size_x, 2)),
            dma((2, 2)),
            dma((size_y, 2)),
            dma((2, 2)),
            dma((2, 2, 2)),
            dma((2, 2, 2)),
        ],
        compiler_params=pltpu.CompilerParams(
            collective_id=0, has_side_effects=True, vmem_limit_bytes=50 * 2**20
        ),
        name="restart",
    )(*operands)


def tile_weights(grid_levels, coefficients, faulty_grids, shape):
    grid_ids = jnp.arange(coefficients.shape[0], dtype=jnp.int32)
    alive = jnp.all(faulty_grids[None, :] != grid_ids[:, None], axis=1)
    share = jnp.where(alive, coefficients, 0).astype(jnp.float32)
    masks = jnp.left_shift(1, grid_levels) - 1
    row = jnp.arange(shape[0], dtype=jnp.int32)
    col = jnp.arange(shape[1], dtype=jnp.int32)
    on_row = (row[None, :] & masks[:, 0:1]) == 0
    on_col = (col[None, :] & masks[:, 1:2]) == 0
    return jnp.sum(
        jnp.where(on_row[:, :, None] & on_col[:, None, :], share[:, None, None], 0.0), axis=0
    )


def local(
    owned_surplus, tile_owner, grid_levels, coefficients, faulty_grids, velocity_x, velocity_y
):
    slot_count, tile_height, tile_width = owned_surplus.shape
    size_x = lax.axis_size("gx")
    size_y = lax.axis_size("gy")
    device_count = size_x * size_y
    capacity = 2 * slot_count // device_count
    own_index = lax.axis_index("gx") * size_y + lax.axis_index("gy")
    offsets = tile_owner[:slot_count]
    positions = jnp.arange(slot_count, dtype=jnp.int32)
    same_offset = offsets[:, None] == offsets[None, :]
    earlier = positions[None, :] < positions[:, None]
    slot_rank = jnp.sum((same_offset & earlier).astype(jnp.int32), axis=1)
    target = (own_index - offsets) % device_count
    seat = target * capacity + slot_rank
    seats = jnp.arange(device_count * capacity, dtype=jnp.int32)
    holder = jnp.max(jnp.where(seat[None, :] == seats[:, None], positions[None, :], 0), axis=1)
    outgoing = jnp.take(owned_surplus, holder, axis=0, mode="clip")
    place = (own_index + offsets) % device_count * capacity + slot_rank
    weight = tile_weights(grid_levels, coefficients, faulty_grids, (tile_height, tile_width))
    return restart(place, weight, outgoing, velocity_x, velocity_y, size_x, size_y)


def solution(mesh):
    return jax.shard_map(
        local,
        mesh=mesh,
        in_specs=(P(("gx", "gy"), None, None), P(), P(), P(), P(), P("gx", "gy"), P("gx", "gy")),
        out_specs=P("gx", "gy"),
        check_vma=False,
    )
```

```python
import functools

import jax
import jax.numpy as jnp
import ml_dtypes
import numpy as np
from jax import lax
from jax.experimental import pallas as pl
from jax.experimental.pallas import tpu as pltpu
from jax.sharding import PartitionSpec as P

STEPS = 2
TIME_STEP = 0.2
CHUNK = 256
HALO = 8
TOP = 16
MESH = pl.DeviceIdType.MESH


def hat_matrix():
    points = np.arange(CHUNK)[:, None]
    nodes = np.arange(CHUNK)[None, :]
    reach = np.where(nodes == 0, 1, nodes & -nodes)
    hats = np.maximum(0.0, 1.0 - np.abs(points - nodes) / reach)
    hats[:, 0] = 0.0
    return hats


def coarse_matrix(count):
    values = np.eye(count)
    spacing = count // 2
    while spacing >= 1:
        for x in range(spacing, count, 2 * spacing):
            values[x] += 0.5 * (values[x - spacing] + values[(x + spacing) % count])
        spacing //= 2
    return values


FIRST = tuple(range(1, 9)) + (16, 32, 64, 128)
LAST = (128, 192, 224, 240) + tuple(range(248, 256))
PACK = 16


def frame_table(size, per_device, length, corner_row, right_row, left_row):
    total = size * per_device
    full = coarse_matrix(total)
    hats = hat_matrix()
    table = np.zeros((size, length, size * 8 + 2 * PACK))
    spots = np.array([(j // per_device) * 8 + j % per_device for j in range(total)])
    for me in range(size):
        for c in range(per_device + 1):
            table[me, corner_row + c, spots] = full[(me * per_device + c) % total]
        for k in range(HALO):
            for row, chunk, point, nodes, start in (
                (right_row + k, (me + 1) * per_device, k, FIRST, size * 8),
                (left_row + k, me * per_device - 1, CHUNK - HALO + k, LAST, size * 8 + PACK),
            ):
                part = point / CHUNK
                table[me, row, spots] = (1 - part) * full[chunk % total] + part * full[
                    (chunk + 1) % total
                ]
                for i, node in enumerate(nodes):
                    table[me, row, start + i] = hats[point, node]
    return table.astype(np.float32)


def split_dot(matrix, values, left):
    high = values.astype(jnp.bfloat16)
    low = (values - high.astype(jnp.float32)).astype(jnp.bfloat16)
    if left:
        return jnp.dot(matrix, high, preferred_element_type=jnp.float32) + jnp.dot(
            matrix, low, preferred_element_type=jnp.float32
        )
    return jnp.dot(high, matrix, preferred_element_type=jnp.float32) + jnp.dot(
        low, matrix, preferred_element_type=jnp.float32
    )


def exact_dot(a, b):
    return jnp.dot(a, b, precision=lax.Precision.HIGHEST, preferred_element_type=jnp.float32)


def kernel(
    size_x,
    size_y,
    owner_ref,
    rank_ref,
    holder_ref,
    levels_ref,
    coefficients_ref,
    faulty_ref,
    owned_ref,
    vel_x_ref,
    vel_y_ref,
    hats_ref,
    hats_t_ref,
    table_x_ref,
    table_y_ref,
    out_ref,
    outgoing,
    incoming,
    block,
    field,
    middle,
    later,
    vel_x,
    vel_y,
    rows_all,
    row_send,
    row_recv,
    cols_all,
    col_send,
    col_recv,
    side_send,
    side_recv,
    local_sem,
    tile_send_sem,
    tile_recv_sem,
    rows_sem,
    row_pack_sem,
    cols_sem,
    col_pack_sem,
    face_sem,
    side_sem,
):
    rows, cols = out_ref.shape
    _, tile_rows, tile_cols = owned_ref.shape
    across = cols // tile_cols
    devices = size_x * size_y
    capacity = incoming.shape[0] // devices
    frame = block.shape[0]
    chunks_x = rows // CHUNK
    chunks_y = cols // CHUNK
    ix = lax.axis_index("gx")
    iy = lax.axis_index("gy")
    me = ix * size_y + iy
    before_x = (lax.rem(ix + size_x - 1, size_x), iy)
    after_x = (lax.rem(ix + 1, size_x), iy)
    before_y = (ix, lax.rem(iy + size_y - 1, size_y))
    after_y = (ix, lax.rem(iy + 1, size_y))

    def remote(src, dst, send_sem, recv_sem, device):
        return pltpu.make_async_remote_copy(
            src_ref=src,
            dst_ref=dst,
            send_sem=send_sem,
            recv_sem=recv_sem,
            device_id=device,
            device_id_type=MESH,
        )

    def partner(step):
        other = lax.rem(me + step, devices)
        return (other // size_y, lax.rem(other, size_y))

    loads = [
        pltpu.make_async_copy(
            source, target.at[pl.ds(TOP, rows), pl.ds(0, cols)], local_sem.at[f]
        )
        for f, source, target in ((0, vel_x_ref, vel_x), (1, vel_y_ref, vel_y))
    ]
    for load in loads:
        load.start()

    barrier = pltpu.get_barrier_semaphore()

    def greet(step, carry):
        pl.semaphore_signal(barrier, inc=1, device_id=partner(step), device_id_type=MESH)
        return carry

    lax.fori_loop(1, devices, greet, 0)
    pl.semaphore_wait(barrier, devices - 1)

    def distance(step):
        return jnp.where(lax.rem(ix, 2) == 0, step, devices - step)

    def tiles_of(device):
        return pl.ds(pl.multiple_of(device * capacity, capacity), capacity)

    def tile_copy(step):
        away = distance(step)
        return remote(
            outgoing.at[tiles_of(lax.rem(me + away, devices))],
            incoming.at[tiles_of(me)],
            tile_send_sem.at[away],
            tile_recv_sem.at[away],
            partner(away),
        )

    def send_tiles(step, carry):
        first = lax.rem(me + distance(step), devices) * capacity
        for i in range(capacity):
            outgoing[first + i] = owned_ref[holder_ref[first + i]]
        tile_copy(step).start()
        return carry

    lax.fori_loop(1, devices, send_tiles, 0)
    for i in range(capacity):
        incoming[me * capacity + i] = owned_ref[holder_ref[me * capacity + i]]

    for load in loads:
        load.wait()
    face_copies = [
        remote(
            vel.at[pl.ds(start, HALO), pl.ds(0, cols)],
            vel.at[pl.ds(target, HALO), pl.ds(0, cols)],
            face_sem.at[f, side, 0],
            face_sem.at[f, side, 1],
            device,
        )
        for f, vel in enumerate((vel_x, vel_y))
        for side, start, target, device in (
            (0, TOP, TOP + rows, before_x),
            (1, TOP + rows - HALO, TOP - HALO, after_x),
        )
    ]
    for copy in face_copies:
        copy.start()

    for copy in face_copies:
        copy.wait()
    side_copies = []
    for f, vel in enumerate((vel_x, vel_y)):
        side_send[f, 0] = vel[:, 0:128].T[0:HALO]
        side_send[f, 1] = vel[:, cols - 128 : cols].T[128 - HALO : 128]
        for side, device in ((0, before_y), (1, after_y)):
            side_copies.append(
                remote(
                    side_send.at[f, side],
                    side_recv.at[f, side],
                    side_sem.at[f, side, 0],
                    side_sem.at[f, side, 1],
                    device,
                )
            )
    for copy in side_copies:
        copy.start()
    row_id = lax.broadcasted_iota(jnp.int32, (tile_rows, tile_cols), 0)
    col_id = lax.broadcasted_iota(jnp.int32, (tile_rows, tile_cols), 1)
    weight = jnp.zeros((tile_rows, tile_cols), jnp.float32)
    for g in range(coefficients_ref.shape[0]):
        share = coefficients_ref[g]
        for i in range(faulty_ref.shape[0]):
            share = jnp.where(faulty_ref[i] == g, 0, share)
        on_row = (row_id & (jnp.left_shift(1, levels_ref[g, 0]) - 1)) == 0
        on_col = (col_id & (jnp.left_shift(1, levels_ref[g, 1]) - 1)) == 0
        weight += jnp.where(on_row & on_col, share.astype(jnp.float32), 0.0)

    def receive_tiles(step, carry):
        tile_copy(step).wait()
        return carry

    lax.fori_loop(1, devices, receive_tiles, 0)

    def put(kx, carry):
        start = pl.multiple_of(TOP + kx * tile_rows, tile_rows)
        for ky in range(across):
            slot = kx * across + ky
            source = me + owner_ref[slot]
            source = jnp.where(source >= devices, source - devices, source)
            block[pl.ds(start, tile_rows), ky * tile_cols : (ky + 1) * tile_cols] = (
                incoming[source * capacity + rank_ref[slot]] * weight
            )
        return carry

    lax.fori_loop(0, rows // tile_rows, put, 0, unroll=2)

    def row(point):
        return block[TOP + point : TOP + point + 1, :]

    def pack_rows(start, nodes):
        return jnp.concatenate(
            [row(start + node) for node in nodes]
            + [jnp.zeros((PACK - len(nodes), cols), jnp.float32)],
            axis=0,
        )

    rows_all[ix] = jnp.concatenate(
        [row(c * CHUNK) for c in range(chunks_x)]
        + [jnp.zeros((8 - chunks_x, cols), jnp.float32)],
        axis=0,
    )
    row_send[0] = pack_rows(0, FIRST)
    row_send[1] = pack_rows(rows - CHUNK, LAST)
    row_copies = [
        remote(
            rows_all.at[ix],
            rows_all.at[ix],
            rows_sem.at[step, 0],
            rows_sem.at[step, 1],
            (lax.rem(ix + step, size_x), iy),
        )
        for step in range(1, size_x)
    ] + [
        remote(
            row_send.at[side],
            row_recv.at[side],
            row_pack_sem.at[side, 0],
            row_pack_sem.at[side, 1],
            device,
        )
        for side, device in ((0, before_x), (1, after_x))
    ]
    for copy in row_copies:
        copy.start()

    for c in range(chunks_x):
        span = slice(TOP + c * CHUNK, TOP + (c + 1) * CHUNK)
        block[span, :] = split_dot(hats_ref[...], block[span, :], True)

    for copy in row_copies:
        copy.wait()
    known = jnp.concatenate(
        [rows_all[...].reshape(size_x * 8, cols), row_recv[...].reshape(2 * PACK, cols)], axis=0
    )
    ends = exact_dot(table_x_ref[ix], known)
    part = lax.broadcasted_iota(jnp.int32, (CHUNK, 1), 0).astype(jnp.float32) * (1.0 / CHUNK)
    for c in range(chunks_x):
        span = slice(TOP + c * CHUNK, TOP + (c + 1) * CHUNK)
        block[span, :] += (1.0 - part) * ends[c : c + 1] + part * ends[c + 1 : c + 2]
    block[TOP + rows : TOP + rows + HALO, :] = ends[8:16]
    block[TOP - HALO : TOP, :] = ends[16:24]

    lane = lax.broadcasted_iota(jnp.int32, (frame, 128), 1)
    picked = block[:, 0:128]
    for spot, point in enumerate([128] + [c * CHUNK for c in range(1, chunks_y)]):
        picked = jnp.where(lane == 10 + spot, block[:, point : point + 1], picked)
    first = picked.T
    last_cols = block[:, cols - 128 : cols].T
    blank = jnp.zeros((8, frame), jnp.float32)
    cols_all[iy] = jnp.concatenate(
        [first[0:1], first[11 : 10 + chunks_y], blank[: 8 - chunks_y]], axis=0
    )
    col_send[0] = jnp.concatenate(
        [first[1:9], first[16:17], first[32:33], first[64:65], first[10:11], blank[:4]], axis=0
    )
    col_send[1] = jnp.concatenate(
        [last_cols[node - 128 : node - 127] for node in LAST] + [blank[:4]], axis=0
    )
    col_copies = [
        remote(
            cols_all.at[iy],
            cols_all.at[iy],
            cols_sem.at[step, 0],
            cols_sem.at[step, 1],
            (ix, lax.rem(iy + step, size_y)),
        )
        for step in range(1, size_y)
    ] + [
        remote(
            col_send.at[side],
            col_recv.at[side],
            col_pack_sem.at[side, 0],
            col_pack_sem.at[side, 1],
            device,
        )
        for side, device in ((0, before_y), (1, after_y))
    ]
    for copy in col_copies:
        copy.start()

    used = rows + 2 * TOP
    for c in range(chunks_y):
        span = slice(c * CHUNK, (c + 1) * CHUNK)
        block[0:used, span] = split_dot(hats_t_ref[...], block[0:used, span], False)

    for copy in side_copies:
        copy.wait()
    for f, vel in enumerate((vel_x, vel_y)):
        strip = jnp.concatenate(
            [
                side_recv[f, 0],
                jnp.zeros((128 - 2 * HALO, frame), jnp.float32),
                side_recv[f, 1],
            ],
            axis=0,
        )
        vel[:, cols : cols + 128] = strip.T

    for copy in col_copies:
        copy.wait()
    known = jnp.concatenate(
        [cols_all[...].reshape(size_y * 8, frame), col_recv[...].reshape(2 * PACK, frame)], axis=0
    )
    ends = exact_dot(table_y_ref[iy], known).T
    field[:, cols : cols + 128] = ends
    part = lax.broadcasted_iota(jnp.int32, (1, CHUNK), 1).astype(jnp.float32) * (1.0 / CHUNK)
    for c in range(chunks_y):
        span = slice(c * CHUNK, (c + 1) * CHUNK)
        field[0:used, span] = (
            block[0:used, span]
            + (1.0 - part) * ends[0:used, 8 + c : 9 + c]
            + part * ends[0:used, 9 + c : 10 + c]
        )

    width = cols + 128
    scale = TIME_STEP / 12.0

    def change(ref, start):
        around = ref.at[pl.ds(pl.multiple_of(start - 8, 8), 24), :]

        def read(shift):
            return around[8 + shift : 16 + shift, :]

        centre = read(0)
        west_one, east_one = read(-1), read(1)
        west_two, east_two = read(-2), read(2)
        north_one = pltpu.roll(centre, width - 1, 1)
        south_one = pltpu.roll(centre, 1, 1)
        north_two = pltpu.roll(centre, width - 2, 1)
        south_two = pltpu.roll(centre, 2, 1)
        near = (east_one + west_one) + (north_one + south_one)
        far = (east_two + west_two) + (north_two + south_two)
        slope_x = 8.0 * (east_one - west_one) - (east_two - west_two)
        slope_y = 8.0 * (north_one - south_one) - (north_two - south_two)
        total = (8.0 * near - 0.5 * far - 30.0 * centre) - (
            vel_x[pl.ds(start, 8), :] * slope_x + vel_y[pl.ds(start, 8), :] * slope_y
        )
        return centre, scale * total

    def sweep(start, count, body):
        def strip(i, carry):
            body(pl.multiple_of(start + i * 8, 8))
            return carry

        group = next(g for g in (8, 6, 4, 3, 2, 1) if count % g == 0)
        lax.fori_loop(0, count, strip, 0, unroll=group)

    now, then = field, later
    for step in range(STEPS):
        last = step == STEPS - 1

        def first_half(start, now=now):
            centre, delta = change(now, start)
            middle[pl.ds(start, 8), :] = centre + delta

        def second_half(start, now=now, then=then, last=last):
            centre, delta = change(middle, start)
            value = 0.5 * (now[pl.ds(start, 8), :] + centre + delta)
            if last:
                out_ref[pl.ds(pl.multiple_of(start - TOP, 8), 8), :] = value[:, :cols]
            else:
                then[pl.ds(start, 8), :] = value

        sweep(TOP - HALO, (rows + 2 * HALO) // 8, first_half)
        if last:
            sweep(TOP, rows // 8, second_half)
        else:
            sweep(TOP - HALO, (rows + 2 * HALO) // 8, second_half)
        now, then = then, now


def restart(scalars, owned, vel_x, vel_y, capacity, size_x, size_y):
    rows, cols = vel_x.shape
    frame = (rows + 2 * TOP + 127) // 128 * 128
    devices = size_x * size_y
    hats = hat_matrix()
    operands = (
        *scalars,
        owned,
        vel_x,
        vel_y,
        jnp.asarray(hats.astype(ml_dtypes.bfloat16)),
        jnp.asarray(hats.T.astype(ml_dtypes.bfloat16)),
        jnp.asarray(frame_table(size_x, rows // CHUNK, 24, 0, 8, 16)),
        jnp.asarray(frame_table(size_y, cols // CHUNK, 128, 8, 0, 120)),
    )
    vmem = pl.BlockSpec(memory_space=pltpu.VMEM)
    smem = pl.BlockSpec(memory_space=pltpu.SMEM)
    tiles = pltpu.VMEM((devices * capacity, *owned.shape[1:]), jnp.float32)
    hbm = pl.BlockSpec(memory_space=pl.ANY)
    dma = pltpu.SemaphoreType.DMA
    framed = pltpu.VMEM((frame, cols + 128), jnp.float32)
    return pl.pallas_call(
        functools.partial(kernel, size_x, size_y),
        out_shape=jax.ShapeDtypeStruct((rows, cols), jnp.float32),
        in_specs=[smem] * len(scalars) + [vmem, hbm, hbm] + [vmem] * 4,
        out_specs=vmem,
        scratch_shapes=[
            tiles,
            tiles,
            pltpu.VMEM((frame, cols), jnp.float32),
            framed,
            framed,
            framed,
            framed,
            framed,
            pltpu.VMEM((size_x, 8, cols), jnp.float32),
            pltpu.VMEM((2, PACK, cols), jnp.float32),
            pltpu.VMEM((2, PACK, cols), jnp.float32),
            pltpu.VMEM((size_y, 8, frame), jnp.float32),
            pltpu.VMEM((2, PACK, frame), jnp.float32),
            pltpu.VMEM((2, PACK, frame), jnp.float32),
            pltpu.VMEM((2, 2, HALO, frame), jnp.float32),
            pltpu.VMEM((2, 2, HALO, frame), jnp.float32),
            dma((3,)),
            dma((devices,)),
            dma((devices,)),
            dma((size_x, 2)),
            dma((2, 2)),
            dma((size_y, 2)),
            dma((2, 2)),
            dma((2, 2, 2)),
            dma((2, 2, 2)),
        ],
        compiler_params=pltpu.CompilerParams(
            collective_id=0, has_side_effects=True, vmem_limit_bytes=50 * 2**20
        ),
        name="restart",
    )(*operands)


def local(
    owned_surplus, tile_owner, grid_levels, coefficients, faulty_grids, velocity_x, velocity_y
):
    slot_count = owned_surplus.shape[0]
    size_x = lax.axis_size("gx")
    size_y = lax.axis_size("gy")
    device_count = size_x * size_y
    capacity = 2 * slot_count // device_count
    own_index = lax.axis_index("gx") * size_y + lax.axis_index("gy")
    offsets = tile_owner[:slot_count]
    positions = jnp.arange(slot_count, dtype=jnp.int32)
    same_offset = offsets[:, None] == offsets[None, :]
    earlier = positions[None, :] < positions[:, None]
    slot_rank = jnp.sum((same_offset & earlier).astype(jnp.int32), axis=1)
    target = (own_index - offsets) % device_count
    seat = target * capacity + slot_rank
    seats = jnp.arange(device_count * capacity, dtype=jnp.int32)
    holder = jnp.max(jnp.where(seat[None, :] == seats[:, None], positions[None, :], 0), axis=1)
    scalars = (tile_owner, slot_rank, holder, grid_levels, coefficients, faulty_grids)
    return restart(scalars, owned_surplus, velocity_x, velocity_y, capacity, size_x, size_y)


def solution(mesh):
    return jax.shard_map(
        local,
        mesh=mesh,
        in_specs=(P(("gx", "gy"), None, None), P(), P(), P(), P(), P("gx", "gy"), P("gx", "gy")),
        out_specs=P("gx", "gy"),
        check_vma=False,
    )
```

```python
import functools

import jax
import jax.numpy as jnp
import ml_dtypes
import numpy as np
from jax import lax
from jax.experimental import pallas as pl
from jax.experimental.pallas import tpu as pltpu
from jax.sharding import PartitionSpec as P

STEPS = 2
TIME_STEP = 0.2
CHUNK = 256
HALO = 8
TOP = 16
MESH = pl.DeviceIdType.MESH


def hat_matrix():
    points = np.arange(CHUNK)[:, None]
    nodes = np.arange(CHUNK)[None, :]
    reach = np.where(nodes == 0, 1, nodes & -nodes)
    hats = np.maximum(0.0, 1.0 - np.abs(points - nodes) / reach)
    hats[:, 0] = 0.0
    return hats


def coarse_matrix(count):
    values = np.eye(count)
    spacing = count // 2
    while spacing >= 1:
        for x in range(spacing, count, 2 * spacing):
            values[x] += 0.5 * (values[x - spacing] + values[(x + spacing) % count])
        spacing //= 2
    return values


FIRST = tuple(range(1, 9)) + (16, 32, 64, 128)
LAST = (128, 192, 224, 240) + tuple(range(248, 256))
PACK = 16


def frame_table(size, per_device, length, corner_row, right_row, left_row):
    total = size * per_device
    full = coarse_matrix(total)
    hats = hat_matrix()
    table = np.zeros((size, length, size * 8 + 2 * PACK))
    spots = np.array([(j // per_device) * 8 + j % per_device for j in range(total)])
    for me in range(size):
        for c in range(per_device + 1):
            table[me, corner_row + c, spots] = full[(me * per_device + c) % total]
        for k in range(HALO):
            for row, chunk, point, nodes, start in (
                (right_row + k, (me + 1) * per_device, k, FIRST, size * 8),
                (left_row + k, me * per_device - 1, CHUNK - HALO + k, LAST, size * 8 + PACK),
            ):
                part = point / CHUNK
                table[me, row, spots] = (1 - part) * full[chunk % total] + part * full[
                    (chunk + 1) % total
                ]
                for i, node in enumerate(nodes):
                    table[me, row, start + i] = hats[point, node]
    return table.astype(np.float32)


def split_dot(matrix, values, left):
    high = values.astype(jnp.bfloat16)
    low = (values - high.astype(jnp.float32)).astype(jnp.bfloat16)
    if left:
        return jnp.dot(matrix, high, preferred_element_type=jnp.float32) + jnp.dot(
            matrix, low, preferred_element_type=jnp.float32
        )
    return jnp.dot(high, matrix, preferred_element_type=jnp.float32) + jnp.dot(
        low, matrix, preferred_element_type=jnp.float32
    )


def exact_dot(a, b):
    return jnp.dot(a, b, precision=lax.Precision.HIGHEST, preferred_element_type=jnp.float32)


def kernel(
    size_x,
    size_y,
    grids,
    faults,
    scalars_ref,
    owned_hbm,
    vel_x_ref,
    vel_y_ref,
    hats_hbm,
    hats_t_hbm,
    table_x_hbm,
    table_y_hbm,
    out_ref,
    owned_ref,
    hats_ref,
    hats_t_ref,
    table_x_ref,
    table_y_ref,
    outgoing,
    incoming,
    block,
    field,
    middle,
    later,
    vel_x,
    vel_y,
    rows_all,
    row_send,
    row_recv,
    cols_all,
    col_send,
    col_recv,
    side_send,
    side_recv,
    local_sem,
    tile_send_sem,
    tile_recv_sem,
    rows_sem,
    row_pack_sem,
    cols_sem,
    col_pack_sem,
    face_sem,
    side_sem,
):
    rows, cols = out_ref.shape
    _, tile_rows, tile_cols = owned_ref.shape
    across = cols // tile_cols
    devices = size_x * size_y
    slots = owned_ref.shape[0]
    capacity = incoming.shape[0] // devices
    seats = devices * capacity
    owner_ref, rank_ref, holder_ref, levels_ref, coefficients_ref, faulty_ref = (
        functools.partial(lambda first, i: scalars_ref[first + i], first)
        for first in (
            0,
            slots,
            2 * slots,
            2 * slots + seats,
            2 * slots + seats + 2 * grids,
            2 * slots + seats + 3 * grids,
        )
    )
    frame = block.shape[0]
    chunks_x = rows // CHUNK
    chunks_y = cols // CHUNK
    ix = lax.axis_index("gx")
    iy = lax.axis_index("gy")
    me = ix * size_y + iy
    before_x = (lax.rem(ix + size_x - 1, size_x), iy)
    after_x = (lax.rem(ix + 1, size_x), iy)
    before_y = (ix, lax.rem(iy + size_y - 1, size_y))
    after_y = (ix, lax.rem(iy + 1, size_y))

    def remote(src, dst, send_sem, recv_sem, device):
        return pltpu.make_async_remote_copy(
            src_ref=src,
            dst_ref=dst,
            send_sem=send_sem,
            recv_sem=recv_sem,
            device_id=device,
            device_id_type=MESH,
        )

    def partner(step):
        other = lax.rem(me + step, devices)
        return (other // size_y, lax.rem(other, size_y))

    loads = [
        pltpu.make_async_copy(
            source, target.at[pl.ds(TOP, rows), pl.ds(0, cols)], local_sem.at[f]
        )
        for f, source, target in ((0, vel_x_ref, vel_x), (1, vel_y_ref, vel_y))
    ]
    tile_load = pltpu.make_async_copy(owned_hbm, owned_ref, local_sem.at[2])
    table_loads = [
        pltpu.make_async_copy(source, target, local_sem.at[3 + f])
        for f, (source, target) in enumerate(
            (
                (hats_hbm, hats_ref),
                (hats_t_hbm, hats_t_ref),
                (table_x_hbm, table_x_ref),
                (table_y_hbm, table_y_ref),
            )
        )
    ]
    for load in [tile_load] + loads + table_loads:
        load.start()

    barrier = pltpu.get_barrier_semaphore()

    def greet(step, carry):
        pl.semaphore_signal(barrier, inc=1, device_id=partner(step), device_id_type=MESH)
        return carry

    lax.fori_loop(1, devices, greet, 0)
    pl.semaphore_wait(barrier, devices - 1)

    def distance(step):
        return jnp.where(lax.rem(ix, 2) == 0, step, devices - step)

    def tiles_of(device):
        return pl.ds(pl.multiple_of(device * capacity, capacity), capacity)

    def tile_copy(step):
        away = distance(step)
        return remote(
            outgoing.at[tiles_of(lax.rem(me + away, devices))],
            incoming.at[tiles_of(me)],
            tile_send_sem.at[away],
            tile_recv_sem.at[away],
            partner(away),
        )

    def send_tiles(step, carry):
        first = lax.rem(me + distance(step), devices) * capacity
        for i in range(capacity):
            outgoing[first + i] = owned_ref[holder_ref(first + i)]
        tile_copy(step).start()
        return carry

    tile_load.wait()
    lax.fori_loop(1, devices, send_tiles, 0)
    for i in range(capacity):
        incoming[me * capacity + i] = owned_ref[holder_ref(me * capacity + i)]

    for load in loads:
        load.wait()
    face_copies = [
        remote(
            vel.at[pl.ds(start, HALO), pl.ds(0, cols)],
            vel.at[pl.ds(target, HALO), pl.ds(0, cols)],
            face_sem.at[f, side, 0],
            face_sem.at[f, side, 1],
            device,
        )
        for f, vel in enumerate((vel_x, vel_y))
        for side, start, target, device in (
            (0, TOP, TOP + rows, before_x),
            (1, TOP + rows - HALO, TOP - HALO, after_x),
        )
    ]
    for copy in face_copies:
        copy.start()

    for copy in face_copies:
        copy.wait()
    scale = TIME_STEP / 12.0

    def scale_rows(i, carry):
        span = pl.ds(pl.multiple_of(TOP - HALO + i * 16, 8), 16)
        for vel in (vel_x, vel_y):
            vel[span, 0:cols] = vel[span, 0:cols] * (8.0 * scale)
        return carry

    lax.fori_loop(0, (rows + 2 * HALO) // 16, scale_rows, 0)
    side_copies = []
    for f, vel in enumerate((vel_x, vel_y)):
        side_send[f, 0] = vel[:, 0:128].T[0:HALO]
        side_send[f, 1] = vel[:, cols - 128 : cols].T[128 - HALO : 128]
        for side, device in ((0, before_y), (1, after_y)):
            side_copies.append(
                remote(
                    side_send.at[f, side],
                    side_recv.at[f, side],
                    side_sem.at[f, side, 0],
                    side_sem.at[f, side, 1],
                    device,
                )
            )
    for copy in side_copies:
        copy.start()
    row_id = lax.broadcasted_iota(jnp.int32, (tile_rows, tile_cols), 0)
    col_id = lax.broadcasted_iota(jnp.int32, (tile_rows, tile_cols), 1)
    weight = jnp.zeros((tile_rows, tile_cols), jnp.float32)
    for g in range(grids):
        share = coefficients_ref(g)
        for i in range(faults):
            share = jnp.where(faulty_ref(i) == g, 0, share)
        on_row = (row_id & (jnp.left_shift(1, levels_ref(2 * g)) - 1)) == 0
        on_col = (col_id & (jnp.left_shift(1, levels_ref(2 * g + 1)) - 1)) == 0
        weight += jnp.where(on_row & on_col, share.astype(jnp.float32), 0.0)

    for load in table_loads:
        load.wait()

    def receive_tiles(step, carry):
        tile_copy(step).wait()
        return carry

    lax.fori_loop(1, devices, receive_tiles, 0)

    def put(kx, carry):
        start = pl.multiple_of(TOP + kx * tile_rows, tile_rows)
        for ky in range(across):
            slot = kx * across + ky
            source = me + owner_ref(slot)
            source = jnp.where(source >= devices, source - devices, source)
            block[pl.ds(start, tile_rows), ky * tile_cols : (ky + 1) * tile_cols] = (
                incoming[source * capacity + rank_ref(slot)] * weight
            )
        return carry

    lax.fori_loop(0, rows // tile_rows, put, 0, unroll=2)

    def row(point):
        return block[TOP + point : TOP + point + 1, :]

    def pack_rows(start, nodes):
        return jnp.concatenate(
            [row(start + node) for node in nodes]
            + [jnp.zeros((PACK - len(nodes), cols), jnp.float32)],
            axis=0,
        )

    rows_all[ix] = jnp.concatenate(
        [row(c * CHUNK) for c in range(chunks_x)]
        + [jnp.zeros((8 - chunks_x, cols), jnp.float32)],
        axis=0,
    )
    row_send[0] = pack_rows(0, FIRST)
    row_send[1] = pack_rows(rows - CHUNK, LAST)
    row_copies = [
        remote(
            rows_all.at[ix],
            rows_all.at[ix],
            rows_sem.at[step, 0],
            rows_sem.at[step, 1],
            (lax.rem(ix + step, size_x), iy),
        )
        for step in range(1, size_x)
    ] + [
        remote(
            row_send.at[side],
            row_recv.at[side],
            row_pack_sem.at[side, 0],
            row_pack_sem.at[side, 1],
            device,
        )
        for side, device in ((0, before_x), (1, after_x))
    ]
    for copy in row_copies:
        copy.start()

    for c in range(chunks_x):
        span = slice(TOP + c * CHUNK, TOP + (c + 1) * CHUNK)
        block[span, :] = split_dot(hats_ref[...], block[span, :], True)

    for copy in row_copies:
        copy.wait()
    known = jnp.concatenate(
        [rows_all[...].reshape(size_x * 8, cols), row_recv[...].reshape(2 * PACK, cols)], axis=0
    )
    ends = exact_dot(table_x_ref[ix], known)
    part = lax.broadcasted_iota(jnp.int32, (CHUNK, 1), 0).astype(jnp.float32) * (1.0 / CHUNK)
    for c in range(chunks_x):
        span = slice(TOP + c * CHUNK, TOP + (c + 1) * CHUNK)
        block[span, :] += (1.0 - part) * ends[c : c + 1] + part * ends[c + 1 : c + 2]
    block[TOP + rows : TOP + rows + HALO, :] = ends[8:16]
    block[TOP - HALO : TOP, :] = ends[16:24]

    lane = lax.broadcasted_iota(jnp.int32, (frame, 128), 1)
    picked = block[:, 0:128]
    for spot, point in enumerate([128] + [c * CHUNK for c in range(1, chunks_y)]):
        picked = jnp.where(lane == 10 + spot, block[:, point : point + 1], picked)
    first = picked.T
    last_cols = block[:, cols - 128 : cols].T
    blank = jnp.zeros((8, frame), jnp.float32)
    cols_all[iy] = jnp.concatenate(
        [first[0:1], first[11 : 10 + chunks_y], blank[: 8 - chunks_y]], axis=0
    )
    col_send[0] = jnp.concatenate(
        [first[1:9], first[16:17], first[32:33], first[64:65], first[10:11], blank[:4]], axis=0
    )
    col_send[1] = jnp.concatenate(
        [last_cols[node - 128 : node - 127] for node in LAST] + [blank[:4]], axis=0
    )
    col_copies = [
        remote(
            cols_all.at[iy],
            cols_all.at[iy],
            cols_sem.at[step, 0],
            cols_sem.at[step, 1],
            (ix, lax.rem(iy + step, size_y)),
        )
        for step in range(1, size_y)
    ] + [
        remote(
            col_send.at[side],
            col_recv.at[side],
            col_pack_sem.at[side, 0],
            col_pack_sem.at[side, 1],
            device,
        )
        for side, device in ((0, before_y), (1, after_y))
    ]
    for copy in col_copies:
        copy.start()

    used = rows + 2 * TOP
    for c in range(chunks_y):
        span = slice(c * CHUNK, (c + 1) * CHUNK)
        block[0:used, span] = split_dot(hats_t_ref[...], block[0:used, span], False)

    for copy in side_copies:
        copy.wait()
    for f, vel in enumerate((vel_x, vel_y)):
        strip = jnp.concatenate(
            [
                side_recv[f, 0],
                jnp.zeros((128 - 2 * HALO, frame), jnp.float32),
                side_recv[f, 1],
            ],
            axis=0,
        )
        vel[:, cols : cols + 128] = strip.T

    for copy in col_copies:
        copy.wait()
    known = jnp.concatenate(
        [cols_all[...].reshape(size_y * 8, frame), col_recv[...].reshape(2 * PACK, frame)], axis=0
    )
    ends = exact_dot(table_y_ref[iy], known).T
    field[:, cols : cols + 128] = ends
    part = lax.broadcasted_iota(jnp.int32, (1, CHUNK), 1).astype(jnp.float32) * (1.0 / CHUNK)
    for c in range(chunks_y):
        span = slice(c * CHUNK, (c + 1) * CHUNK)
        field[0:used, span] = (
            block[0:used, span]
            + (1.0 - part) * ends[0:used, 8 + c : 9 + c]
            + part * ends[0:used, 9 + c : 10 + c]
        )

    width = cols + 128
    group = 16

    def advance(ref, start):
        around = ref.at[pl.ds(pl.multiple_of(start - 8, 8), group + 16), :]

        def read(shift):
            return around[8 + shift : 8 + group + shift, :]

        centre = read(0)
        west_one, east_one = read(-1), read(1)
        west_two, east_two = read(-2), read(2)
        north_one = pltpu.roll(centre, width - 1, 1)
        south_one = pltpu.roll(centre, 1, 1)
        north_two = pltpu.roll(centre, width - 2, 1)
        south_two = pltpu.roll(centre, 2, 1)
        near = (east_one + west_one) + (north_one + south_one)
        far = (east_two + west_two) + (north_two + south_two)
        slope_x = (east_one - west_one) - 0.125 * (east_two - west_two)
        slope_y = (north_one - south_one) - 0.125 * (north_two - south_two)
        span = pl.ds(start, group)
        moved = vel_x[span, :] * slope_x + vel_y[span, :] * slope_y
        return (
            (1.0 - 30.0 * scale) * centre + ((8.0 * scale) * near - (0.5 * scale) * far) - moved
        )

    def sweep(start, count, body):
        def strip(i, carry):
            body(pl.multiple_of(start + i * group, 8))
            return carry

        unroll = next(g for g in (4, 3, 2, 1) if count % g == 0)
        lax.fori_loop(0, count, strip, 0, unroll=unroll)

    now, then = field, later
    for step in range(STEPS):
        last = step == STEPS - 1

        def first_half(start, now=now):
            middle[pl.ds(start, group), :] = advance(now, start)

        def second_half(start, now=now, then=then, last=last):
            value = 0.5 * (now[pl.ds(start, group), :] + advance(middle, start))
            if last:
                out_ref[pl.ds(pl.multiple_of(start - TOP, 8), group), :] = value[:, :cols]
            else:
                then[pl.ds(start, group), :] = value

        sweep(TOP - HALO, (rows + 2 * HALO) // group, first_half)
        if last:
            sweep(TOP, rows // group, second_half)
        else:
            sweep(TOP - HALO, (rows + 2 * HALO) // group, second_half)
        now, then = then, now


def restart(scalars, owned, vel_x, vel_y, capacity, grids, faults, size_x, size_y):
    rows, cols = vel_x.shape
    frame = (rows + 2 * TOP + 127) // 128 * 128
    devices = size_x * size_y
    hats = hat_matrix()
    tables = (
        jnp.asarray(hats.astype(ml_dtypes.bfloat16)),
        jnp.asarray(hats.T.astype(ml_dtypes.bfloat16)),
        jnp.asarray(frame_table(size_x, rows // CHUNK, 24, 0, 8, 16)),
        jnp.asarray(frame_table(size_y, cols // CHUNK, 128, 8, 0, 120)),
    )
    operands = (scalars, owned, vel_x, vel_y, *tables)
    vmem = pl.BlockSpec(memory_space=pltpu.VMEM)
    smem = pl.BlockSpec(memory_space=pltpu.SMEM)
    tiles = pltpu.VMEM((devices * capacity, *owned.shape[1:]), jnp.float32)
    hbm = pl.BlockSpec(memory_space=pl.ANY)
    dma = pltpu.SemaphoreType.DMA
    framed = pltpu.VMEM((frame, cols + 128), jnp.float32)
    return pl.pallas_call(
        functools.partial(kernel, size_x, size_y, grids, faults),
        out_shape=jax.ShapeDtypeStruct((rows, cols), jnp.float32),
        in_specs=[smem] + [hbm] * 7,
        out_specs=vmem,
        scratch_shapes=[
            pltpu.VMEM(owned.shape, jnp.float32),
            *(pltpu.VMEM(table.shape, table.dtype) for table in tables),
            tiles,
            tiles,
            pltpu.VMEM((frame, cols), jnp.float32),
            framed,
            framed,
            framed,
            framed,
            framed,
            pltpu.VMEM((size_x, 8, cols), jnp.float32),
            pltpu.VMEM((2, PACK, cols), jnp.float32),
            pltpu.VMEM((2, PACK, cols), jnp.float32),
            pltpu.VMEM((size_y, 8, frame), jnp.float32),
            pltpu.VMEM((2, PACK, frame), jnp.float32),
            pltpu.VMEM((2, PACK, frame), jnp.float32),
            pltpu.VMEM((2, 2, HALO, frame), jnp.float32),
            pltpu.VMEM((2, 2, HALO, frame), jnp.float32),
            dma((7,)),
            dma((devices,)),
            dma((devices,)),
            dma((size_x, 2)),
            dma((2, 2)),
            dma((size_y, 2)),
            dma((2, 2)),
            dma((2, 2, 2)),
            dma((2, 2, 2)),
        ],
        compiler_params=pltpu.CompilerParams(
            collective_id=0, has_side_effects=True, vmem_limit_bytes=50 * 2**20
        ),
        name="restart",
    )(*operands)


def local(
    owned_surplus, tile_owner, grid_levels, coefficients, faulty_grids, velocity_x, velocity_y
):
    slot_count = owned_surplus.shape[0]
    size_x = lax.axis_size("gx")
    size_y = lax.axis_size("gy")
    device_count = size_x * size_y
    capacity = 2 * slot_count // device_count
    own_index = lax.axis_index("gx") * size_y + lax.axis_index("gy")
    offsets = tile_owner[:slot_count]
    positions = jnp.arange(slot_count, dtype=jnp.int32)
    same_offset = offsets[:, None] == offsets[None, :]
    earlier = positions[None, :] < positions[:, None]
    slot_rank = jnp.sum((same_offset & earlier).astype(jnp.int32), axis=1)
    target = (own_index - offsets) % device_count
    seat = target * capacity + slot_rank
    seats = jnp.arange(device_count * capacity, dtype=jnp.int32)
    holder = jnp.max(jnp.where(seat[None, :] == seats[:, None], positions[None, :], 0), axis=1)
    scalars = jnp.concatenate(
        [offsets, slot_rank, holder, grid_levels.reshape(-1), coefficients, faulty_grids]
    )
    return restart(
        scalars,
        owned_surplus,
        velocity_x,
        velocity_y,
        capacity,
        coefficients.shape[0],
        faulty_grids.shape[0],
        size_x,
        size_y,
    )


def solution(mesh):
    return jax.shard_map(
        local,
        mesh=mesh,
        in_specs=(P(("gx", "gy"), None, None), P(), P(), P(), P(), P("gx", "gy"), P("gx", "gy")),
        out_specs=P("gx", "gy"),
        check_vma=False,
    )
```

```python
import functools

import jax
import jax.numpy as jnp
import numpy as np
from jax import lax
from jax.experimental import pallas as pl
from jax.experimental.pallas import tpu as pltpu
from jax.sharding import PartitionSpec as P

STEPS = 2
TIME_STEP = 0.2
CHUNK = 256
HALO = 8
TOP = 16
MESH = pl.DeviceIdType.MESH


def hat_matrix():
    points = np.arange(CHUNK)[:, None]
    nodes = np.arange(CHUNK)[None, :]
    reach = np.where(nodes == 0, 1, nodes & -nodes)
    hats = np.maximum(0.0, 1.0 - np.abs(points - nodes) / reach)
    hats[:, 0] = 0.0
    return hats


def coarse_matrix(count):
    values = np.eye(count)
    spacing = count // 2
    while spacing >= 1:
        for x in range(spacing, count, 2 * spacing):
            values[x] += 0.5 * (values[x - spacing] + values[(x + spacing) % count])
        spacing //= 2
    return values


FIRST = tuple(range(1, 9)) + (16, 32, 64, 128)
LAST = (128, 192, 224, 240) + tuple(range(248, 256))
PACK = 16


def frame_table(size, per_device, length, corner_row, right_row, left_row):
    total = size * per_device
    full = coarse_matrix(total)
    hats = hat_matrix()
    table = np.zeros((size, length, size * 8 + 2 * PACK))
    spots = np.array([(j // per_device) * 8 + j % per_device for j in range(total)])
    for me in range(size):
        for c in range(per_device + 1):
            table[me, corner_row + c, spots] = full[(me * per_device + c) % total]
        for k in range(HALO):
            for row, chunk, point, nodes, start in (
                (right_row + k, (me + 1) * per_device, k, FIRST, size * 8),
                (left_row + k, me * per_device - 1, CHUNK - HALO + k, LAST, size * 8 + PACK),
            ):
                part = point / CHUNK
                table[me, row, spots] = (1 - part) * full[chunk % total] + part * full[
                    (chunk + 1) % total
                ]
                for i, node in enumerate(nodes):
                    table[me, row, start + i] = hats[point, node]
    return table.astype(np.float32)


def hats_of(points_dim):
    points = lax.broadcasted_iota(jnp.int32, (CHUNK, CHUNK), points_dim)
    nodes = lax.broadcasted_iota(jnp.int32, (CHUNK, CHUNK), 1 - points_dim)
    slope = jnp.ones((CHUNK, CHUNK), jnp.float32)
    reach = 2
    while reach < CHUNK:
        slope = jnp.where((nodes & (reach - 1)) == 0, 1.0 / reach, slope)
        reach *= 2
    hats = jnp.maximum(1.0 - jnp.abs(points - nodes).astype(jnp.float32) * slope, 0.0)
    return jnp.where(nodes == 0, 0.0, hats).astype(jnp.bfloat16)


def split_dot(matrix, values, left):
    high = values.astype(jnp.bfloat16)
    low = (values - high.astype(jnp.float32)).astype(jnp.bfloat16)
    if left:
        return jnp.dot(matrix, high, preferred_element_type=jnp.float32) + jnp.dot(
            matrix, low, preferred_element_type=jnp.float32
        )
    return jnp.dot(high, matrix, preferred_element_type=jnp.float32) + jnp.dot(
        low, matrix, preferred_element_type=jnp.float32
    )


def exact_dot(a, b):
    return jnp.dot(a, b, precision=lax.Precision.HIGHEST, preferred_element_type=jnp.float32)


def kernel(
    size_x,
    size_y,
    grids,
    faults,
    scalars_ref,
    owned_hbm,
    vel_x_ref,
    vel_y_ref,
    tables_hbm,
    out_ref,
    owned_ref,
    hats_ref,
    hats_t_ref,
    tables_ref,
    outgoing,
    incoming,
    block,
    field,
    middle,
    later,
    vel_x,
    vel_y,
    rows_all,
    row_send,
    row_recv,
    cols_all,
    col_send,
    col_recv,
    side_send,
    side_recv,
    local_sem,
    tile_send_sem,
    tile_recv_sem,
    rows_sem,
    row_pack_sem,
    cols_sem,
    col_pack_sem,
    face_sem,
    side_sem,
):
    rows, cols = out_ref.shape
    _, tile_rows, tile_cols = owned_ref.shape
    across = cols // tile_cols
    devices = size_x * size_y
    slots = owned_ref.shape[0]
    capacity = incoming.shape[0] // devices
    seats = devices * capacity
    owner_ref, rank_ref, holder_ref, levels_ref, coefficients_ref, faulty_ref = (
        functools.partial(lambda first, i: scalars_ref[first + i], first)
        for first in (
            0,
            slots,
            2 * slots,
            2 * slots + seats,
            2 * slots + seats + 2 * grids,
            2 * slots + seats + 3 * grids,
        )
    )
    frame = block.shape[0]
    chunks_x = rows // CHUNK
    chunks_y = cols // CHUNK
    ix = lax.axis_index("gx")
    iy = lax.axis_index("gy")
    me = ix * size_y + iy
    before_x = (lax.rem(ix + size_x - 1, size_x), iy)
    after_x = (lax.rem(ix + 1, size_x), iy)
    before_y = (ix, lax.rem(iy + size_y - 1, size_y))
    after_y = (ix, lax.rem(iy + 1, size_y))

    def remote(src, dst, send_sem, recv_sem, device):
        return pltpu.make_async_remote_copy(
            src_ref=src,
            dst_ref=dst,
            send_sem=send_sem,
            recv_sem=recv_sem,
            device_id=device,
            device_id_type=MESH,
        )

    def partner(step):
        other = lax.rem(me + step, devices)
        return (other // size_y, lax.rem(other, size_y))

    loads = [
        pltpu.make_async_copy(
            source, target.at[pl.ds(TOP, rows), pl.ds(0, cols)], local_sem.at[f]
        )
        for f, source, target in ((0, vel_x_ref, vel_x), (1, vel_y_ref, vel_y))
    ]
    tile_load = pltpu.make_async_copy(owned_hbm, owned_ref, local_sem.at[2])
    table_loads = [pltpu.make_async_copy(tables_hbm, tables_ref, local_sem.at[3])]
    for load in [tile_load] + loads + table_loads:
        load.start()

    barrier = pltpu.get_barrier_semaphore()

    def greet(step, carry):
        pl.semaphore_signal(barrier, inc=1, device_id=partner(step), device_id_type=MESH)
        return carry

    lax.fori_loop(1, devices, greet, 0)
    pl.semaphore_wait(barrier, devices - 1)

    def distance(step):
        return jnp.where(lax.rem(ix, 2) == 0, step, devices - step)

    def tiles_of(device):
        return pl.ds(pl.multiple_of(device * capacity, capacity), capacity)

    def tile_copy(step):
        away = distance(step)
        return remote(
            outgoing.at[tiles_of(lax.rem(me + away, devices))],
            incoming.at[tiles_of(me)],
            tile_send_sem.at[away],
            tile_recv_sem.at[away],
            partner(away),
        )

    def send_tiles(step, carry):
        first = lax.rem(me + distance(step), devices) * capacity
        for i in range(capacity):
            outgoing[first + i] = owned_ref[holder_ref(first + i)]
        tile_copy(step).start()
        return carry

    tile_load.wait()
    lax.fori_loop(1, devices, send_tiles, 0)
    for i in range(capacity):
        incoming[me * capacity + i] = owned_ref[holder_ref(me * capacity + i)]

    for load in loads:
        load.wait()
    face_copies = [
        remote(
            vel.at[pl.ds(start, HALO), pl.ds(0, cols)],
            vel.at[pl.ds(target, HALO), pl.ds(0, cols)],
            face_sem.at[f, side, 0],
            face_sem.at[f, side, 1],
            device,
        )
        for f, vel in enumerate((vel_x, vel_y))
        for side, start, target, device in (
            (0, TOP, TOP + rows, before_x),
            (1, TOP + rows - HALO, TOP - HALO, after_x),
        )
    ]
    for copy in face_copies:
        copy.start()

    for copy in face_copies:
        copy.wait()
    scale = TIME_STEP / 12.0

    def scale_rows(i, carry):
        span = pl.ds(pl.multiple_of(TOP - HALO + i * 16, 8), 16)
        for vel in (vel_x, vel_y):
            vel[span, 0:cols] = vel[span, 0:cols] * (8.0 * scale)
        return carry

    lax.fori_loop(0, (rows + 2 * HALO) // 16, scale_rows, 0)
    side_copies = []
    for f, vel in enumerate((vel_x, vel_y)):
        side_send[f, 0] = vel[:, 0:128].T[0:HALO]
        side_send[f, 1] = vel[:, cols - 128 : cols].T[128 - HALO : 128]
        for side, device in ((0, before_y), (1, after_y)):
            side_copies.append(
                remote(
                    side_send.at[f, side],
                    side_recv.at[f, side],
                    side_sem.at[f, side, 0],
                    side_sem.at[f, side, 1],
                    device,
                )
            )
    for copy in side_copies:
        copy.start()
    row_id = lax.broadcasted_iota(jnp.int32, (tile_rows, tile_cols), 0)
    col_id = lax.broadcasted_iota(jnp.int32, (tile_rows, tile_cols), 1)
    weight = jnp.zeros((tile_rows, tile_cols), jnp.float32)
    for g in range(grids):
        share = coefficients_ref(g)
        for i in range(faults):
            share = jnp.where(faulty_ref(i) == g, 0, share)
        on_row = (row_id & (jnp.left_shift(1, levels_ref(g)) - 1)) == 0
        on_col = (col_id & (jnp.left_shift(1, levels_ref(grids + g)) - 1)) == 0
        weight += jnp.where(on_row & on_col, share.astype(jnp.float32), 0.0)

    for load in table_loads:
        load.wait()
    hats_ref[...] = hats_of(0)
    hats_t_ref[...] = hats_of(1)

    def receive_tiles(step, carry):
        tile_copy(step).wait()
        return carry

    lax.fori_loop(1, devices, receive_tiles, 0)

    def put(kx, carry):
        start = pl.multiple_of(TOP + kx * tile_rows, tile_rows)
        for ky in range(across):
            slot = kx * across + ky
            source = me + owner_ref(slot)
            source = jnp.where(source >= devices, source - devices, source)
            block[pl.ds(start, tile_rows), ky * tile_cols : (ky + 1) * tile_cols] = (
                incoming[source * capacity + rank_ref(slot)] * weight
            )
        return carry

    lax.fori_loop(0, rows // tile_rows, put, 0, unroll=2)

    def row(point):
        return block[TOP + point : TOP + point + 1, :]

    def pack_rows(start, nodes):
        return jnp.concatenate(
            [row(start + node) for node in nodes]
            + [jnp.zeros((PACK - len(nodes), cols), jnp.float32)],
            axis=0,
        )

    rows_all[ix] = jnp.concatenate(
        [row(c * CHUNK) for c in range(chunks_x)]
        + [jnp.zeros((8 - chunks_x, cols), jnp.float32)],
        axis=0,
    )
    row_send[0] = pack_rows(0, FIRST)
    row_send[1] = pack_rows(rows - CHUNK, LAST)
    row_copies = [
        remote(
            rows_all.at[ix],
            rows_all.at[ix],
            rows_sem.at[step, 0],
            rows_sem.at[step, 1],
            (lax.rem(ix + step, size_x), iy),
        )
        for step in range(1, size_x)
    ] + [
        remote(
            row_send.at[side],
            row_recv.at[side],
            row_pack_sem.at[side, 0],
            row_pack_sem.at[side, 1],
            device,
        )
        for side, device in ((0, before_x), (1, after_x))
    ]
    for copy in row_copies:
        copy.start()

    for c in range(chunks_x):
        span = slice(TOP + c * CHUNK, TOP + (c + 1) * CHUNK)
        block[span, :] = split_dot(hats_ref[...], block[span, :], True)

    for copy in row_copies:
        copy.wait()
    known = jnp.concatenate(
        [rows_all[...].reshape(size_x * 8, cols), row_recv[...].reshape(2 * PACK, cols)], axis=0
    )
    ends = exact_dot(tables_ref[pl.ds(size_y * 128 + ix * 24, 24), 0 : size_x * 8 + 2 * PACK], known)
    part = lax.broadcasted_iota(jnp.int32, (CHUNK, 1), 0).astype(jnp.float32) * (1.0 / CHUNK)
    for c in range(chunks_x):
        span = slice(TOP + c * CHUNK, TOP + (c + 1) * CHUNK)
        block[span, :] += (1.0 - part) * ends[c : c + 1] + part * ends[c + 1 : c + 2]
    block[TOP + rows : TOP + rows + HALO, :] = ends[8:16]
    block[TOP - HALO : TOP, :] = ends[16:24]

    lane = lax.broadcasted_iota(jnp.int32, (frame, 128), 1)
    picked = block[:, 0:128]
    for spot, point in enumerate([128] + [c * CHUNK for c in range(1, chunks_y)]):
        picked = jnp.where(lane == 10 + spot, block[:, point : point + 1], picked)
    first = picked.T
    last_cols = block[:, cols - 128 : cols].T
    blank = jnp.zeros((8, frame), jnp.float32)
    cols_all[iy] = jnp.concatenate(
        [first[0:1], first[11 : 10 + chunks_y], blank[: 8 - chunks_y]], axis=0
    )
    col_send[0] = jnp.concatenate(
        [first[1:9], first[16:17], first[32:33], first[64:65], first[10:11], blank[:4]], axis=0
    )
    col_send[1] = jnp.concatenate(
        [last_cols[node - 128 : node - 127] for node in LAST] + [blank[:4]], axis=0
    )
    col_copies = [
        remote(
            cols_all.at[iy],
            cols_all.at[iy],
            cols_sem.at[step, 0],
            cols_sem.at[step, 1],
            (ix, lax.rem(iy + step, size_y)),
        )
        for step in range(1, size_y)
    ] + [
        remote(
            col_send.at[side],
            col_recv.at[side],
            col_pack_sem.at[side, 0],
            col_pack_sem.at[side, 1],
            device,
        )
        for side, device in ((0, before_y), (1, after_y))
    ]
    for copy in col_copies:
        copy.start()

    used = rows + 2 * TOP
    for c in range(chunks_y):
        span = slice(c * CHUNK, (c + 1) * CHUNK)
        block[0:used, span] = split_dot(hats_t_ref[...], block[0:used, span], False)

    for copy in side_copies:
        copy.wait()
    for f, vel in enumerate((vel_x, vel_y)):
        strip = jnp.concatenate(
            [
                side_recv[f, 0],
                jnp.zeros((128 - 2 * HALO, frame), jnp.float32),
                side_recv[f, 1],
            ],
            axis=0,
        )
        vel[:, cols : cols + 128] = strip.T

    for copy in col_copies:
        copy.wait()
    known = jnp.concatenate(
        [cols_all[...].reshape(size_y * 8, frame), col_recv[...].reshape(2 * PACK, frame)], axis=0
    )
    ends = exact_dot(tables_ref[pl.ds(iy * 128, 128), :], known).T
    field[:, cols : cols + 128] = ends
    part = lax.broadcasted_iota(jnp.int32, (1, CHUNK), 1).astype(jnp.float32) * (1.0 / CHUNK)
    for c in range(chunks_y):
        span = slice(c * CHUNK, (c + 1) * CHUNK)
        field[0:used, span] = (
            block[0:used, span]
            + (1.0 - part) * ends[0:used, 8 + c : 9 + c]
            + part * ends[0:used, 9 + c : 10 + c]
        )

    width = cols + 128

    def advance(ref, start, group):
        around = ref.at[pl.ds(pl.multiple_of(start - 8, 8), group + 16), :]

        def read(shift):
            return around[8 + shift : 8 + group + shift, :]

        centre = read(0)
        west_one, east_one = read(-1), read(1)
        west_two, east_two = read(-2), read(2)
        north_one = pltpu.roll(centre, width - 1, 1)
        south_one = pltpu.roll(centre, 1, 1)
        north_two = pltpu.roll(centre, width - 2, 1)
        south_two = pltpu.roll(centre, 2, 1)
        near = (east_one + west_one) + (north_one + south_one)
        far = (east_two + west_two) + (north_two + south_two)
        slope_x = (east_one - west_one) - 0.125 * (east_two - west_two)
        slope_y = (north_one - south_one) - 0.125 * (north_two - south_two)
        span = pl.ds(start, group)
        moved = vel_x[span, :] * slope_x + vel_y[span, :] * slope_y
        return (
            (1.0 - 30.0 * scale) * centre + ((8.0 * scale) * near - (0.5 * scale) * far) - moved
        )

    def sweep(start, length, body):
        group = next(g for g in (48, 32, 16, 8) if length % g == 0)

        def strip(i, carry):
            body(pl.multiple_of(start + i * group, 8), group)
            return carry

        lax.fori_loop(0, length // group, strip, 0)

    now, then = field, later
    for step in range(STEPS):
        last = step == STEPS - 1

        def first_half(start, group, now=now):
            middle[pl.ds(start, group), :] = advance(now, start, group)

        def second_half(start, group, now=now, then=then, last=last):
            value = 0.5 * (now[pl.ds(start, group), :] + advance(middle, start, group))
            if last:
                out_ref[pl.ds(pl.multiple_of(start - TOP, 8), group), :] = value[:, :cols]
            else:
                then[pl.ds(start, group), :] = value

        sweep(TOP - HALO, rows + 2 * HALO, first_half)
        if last:
            sweep(TOP, rows, second_half)
        else:
            sweep(TOP - HALO, rows + 2 * HALO, second_half)
        now, then = then, now


def restart(scalars, owned, vel_x, vel_y, capacity, grids, faults, size_x, size_y):
    rows, cols = vel_x.shape
    frame = (rows + 2 * TOP + 127) // 128 * 128
    devices = size_x * size_y
    table_x = frame_table(size_x, rows // CHUNK, 24, 0, 8, 16)
    table_y = frame_table(size_y, cols // CHUNK, 128, 8, 0, 120)
    wider = table_y.shape[2] - table_x.shape[2]
    table_x = np.pad(table_x, ((0, 0), (0, 0), (0, wider)))
    tables = jnp.asarray(
        np.concatenate([table.reshape(-1, table.shape[2]) for table in (table_y, table_x)])
    )
    operands = (scalars, owned, vel_x, vel_y, tables)
    vmem = pl.BlockSpec(memory_space=pltpu.VMEM)
    smem = pl.BlockSpec(memory_space=pltpu.SMEM)
    tiles = pltpu.VMEM((devices * capacity, *owned.shape[1:]), jnp.float32)
    hbm = pl.BlockSpec(memory_space=pl.ANY)
    dma = pltpu.SemaphoreType.DMA
    framed = pltpu.VMEM((frame, cols + 128), jnp.float32)
    return pl.pallas_call(
        functools.partial(kernel, size_x, size_y, grids, faults),
        out_shape=jax.ShapeDtypeStruct((rows, cols), jnp.float32),
        in_specs=[smem] + [hbm] * 4,
        out_specs=vmem,
        scratch_shapes=[
            pltpu.VMEM(owned.shape, jnp.float32),
            pltpu.VMEM((CHUNK, CHUNK), jnp.bfloat16),
            pltpu.VMEM((CHUNK, CHUNK), jnp.bfloat16),
            pltpu.VMEM(tables.shape, jnp.float32),
            tiles,
            tiles,
            pltpu.VMEM((frame, cols), jnp.float32),
            framed,
            framed,
            framed,
            framed,
            framed,
            pltpu.VMEM((size_x, 8, cols), jnp.float32),
            pltpu.VMEM((2, PACK, cols), jnp.float32),
            pltpu.VMEM((2, PACK, cols), jnp.float32),
            pltpu.VMEM((size_y, 8, frame), jnp.float32),
            pltpu.VMEM((2, PACK, frame), jnp.float32),
            pltpu.VMEM((2, PACK, frame), jnp.float32),
            pltpu.VMEM((2, 2, HALO, frame), jnp.float32),
            pltpu.VMEM((2, 2, HALO, frame), jnp.float32),
            dma((4,)),
            dma((devices,)),
            dma((devices,)),
            dma((size_x, 2)),
            dma((2, 2)),
            dma((size_y, 2)),
            dma((2, 2)),
            dma((2, 2, 2)),
            dma((2, 2, 2)),
        ],
        compiler_params=pltpu.CompilerParams(
            collective_id=0, has_side_effects=True, vmem_limit_bytes=50 * 2**20
        ),
        name="restart",
    )(*operands)


def local(
    owned_surplus, tile_owner, grid_levels, coefficients, faulty_grids, velocity_x, velocity_y
):
    slot_count = owned_surplus.shape[0]
    size_x = lax.axis_size("gx")
    size_y = lax.axis_size("gy")
    device_count = size_x * size_y
    capacity = 2 * slot_count // device_count
    own_index = lax.axis_index("gx") * size_y + lax.axis_index("gy")
    offsets = tile_owner[:slot_count]
    positions = jnp.arange(slot_count, dtype=jnp.int32)
    same_offset = offsets[:, None] == offsets[None, :]
    earlier = positions[None, :] < positions[:, None]
    slot_rank = jnp.sum((same_offset & earlier).astype(jnp.int32), axis=1)
    target = (own_index - offsets) % device_count
    seat = target * capacity + slot_rank
    seats = jnp.arange(device_count * capacity, dtype=jnp.int32)
    holder = jnp.max(jnp.where(seat[None, :] == seats[:, None], positions[None, :], 0), axis=1)
    scalars = jnp.concatenate(
        [offsets, slot_rank, holder, grid_levels.T.reshape(-1), coefficients, faulty_grids]
    )
    return restart(
        scalars,
        owned_surplus,
        velocity_x,
        velocity_y,
        capacity,
        coefficients.shape[0],
        faulty_grids.shape[0],
        size_x,
        size_y,
    )


def solution(mesh):
    return jax.shard_map(
        local,
        mesh=mesh,
        in_specs=(P(("gx", "gy"), None, None), P(), P(), P(), P(), P("gx", "gy"), P("gx", "gy")),
        out_specs=P("gx", "gy"),
        check_vma=False,
    )
```

```python
import functools

import jax
import jax.numpy as jnp
import numpy as np
from jax import lax
from jax.experimental import pallas as pl
from jax.experimental.pallas import tpu as pltpu
from jax.sharding import PartitionSpec as P

STEPS = 2
TIME_STEP = 0.2
CHUNK = 256
HALO = 8
TOP = 16
MESH = pl.DeviceIdType.MESH


def hat_matrix():
    points = np.arange(CHUNK)[:, None]
    nodes = np.arange(CHUNK)[None, :]
    reach = np.where(nodes == 0, 1, nodes & -nodes)
    hats = np.maximum(0.0, 1.0 - np.abs(points - nodes) / reach)
    hats[:, 0] = 0.0
    return hats


def coarse_matrix(count):
    values = np.eye(count)
    spacing = count // 2
    while spacing >= 1:
        for x in range(spacing, count, 2 * spacing):
            values[x] += 0.5 * (values[x - spacing] + values[(x + spacing) % count])
        spacing //= 2
    return values


FIRST = tuple(range(1, 9)) + (16, 32, 64, 128)
LAST = (128, 192, 224, 240) + tuple(range(248, 256))
PACK = 16


def frame_table(size, per_device, length, corner_row, right_row, left_row):
    total = size * per_device
    full = coarse_matrix(total)
    hats = hat_matrix()
    table = np.zeros((size, length, size * 8 + 2 * PACK))
    spots = np.array([(j // per_device) * 8 + j % per_device for j in range(total)])
    for me in range(size):
        for c in range(per_device + 1):
            table[me, corner_row + c, spots] = full[(me * per_device + c) % total]
        for k in range(HALO):
            for row, chunk, point, nodes, start in (
                (right_row + k, (me + 1) * per_device, k, FIRST, size * 8),
                (left_row + k, me * per_device - 1, CHUNK - HALO + k, LAST, size * 8 + PACK),
            ):
                part = point / CHUNK
                table[me, row, spots] = (1 - part) * full[chunk % total] + part * full[
                    (chunk + 1) % total
                ]
                for i, node in enumerate(nodes):
                    table[me, row, start + i] = hats[point, node]
    return table.astype(np.float32)


def hats_of(points_dim):
    points = lax.broadcasted_iota(jnp.int32, (CHUNK, CHUNK), points_dim)
    nodes = lax.broadcasted_iota(jnp.int32, (CHUNK, CHUNK), 1 - points_dim)
    slope = jnp.ones((CHUNK, CHUNK), jnp.float32)
    reach = 2
    while reach < CHUNK:
        slope = jnp.where((nodes & (reach - 1)) == 0, 1.0 / reach, slope)
        reach *= 2
    hats = jnp.maximum(1.0 - jnp.abs(points - nodes).astype(jnp.float32) * slope, 0.0)
    return jnp.where(nodes == 0, 0.0, hats).astype(jnp.bfloat16)


def split_dot(matrix, values, left):
    high = values.astype(jnp.bfloat16)
    low = (values - high.astype(jnp.float32)).astype(jnp.bfloat16)
    if left:
        return jnp.dot(matrix, high, preferred_element_type=jnp.float32) + jnp.dot(
            matrix, low, preferred_element_type=jnp.float32
        )
    return jnp.dot(high, matrix, preferred_element_type=jnp.float32) + jnp.dot(
        low, matrix, preferred_element_type=jnp.float32
    )


def exact_dot(a, b):
    return jnp.dot(a, b, precision=lax.Precision.HIGHEST, preferred_element_type=jnp.float32)


def kernel(
    size_x,
    size_y,
    grids,
    faults,
    scalars_ref,
    owned_hbm,
    vel_x_ref,
    vel_y_ref,
    tables_hbm,
    out_ref,
    owned_ref,
    hats_ref,
    hats_t_ref,
    tables_ref,
    outgoing,
    incoming,
    block,
    field,
    middle,
    later,
    vel_x,
    vel_y,
    rows_all,
    row_send,
    row_recv,
    cols_all,
    col_send,
    col_recv,
    side_send,
    side_recv,
    local_sem,
    tile_send_sem,
    tile_recv_sem,
    rows_sem,
    row_pack_sem,
    cols_sem,
    col_pack_sem,
    face_sem,
    side_sem,
):
    rows, cols = out_ref.shape
    _, tile_rows, tile_cols = owned_ref.shape
    across = cols // tile_cols
    devices = size_x * size_y
    slots = owned_ref.shape[0]
    capacity = incoming.shape[0] // devices
    seats = devices * capacity
    owner_ref, rank_ref, holder_ref, levels_ref, coefficients_ref, faulty_ref = (
        functools.partial(lambda first, i: scalars_ref[first + i], first)
        for first in (
            0,
            slots,
            2 * slots,
            2 * slots + seats,
            2 * slots + seats + 2 * grids,
            2 * slots + seats + 3 * grids,
        )
    )
    frame = block.shape[0]
    chunks_x = rows // CHUNK
    chunks_y = cols // CHUNK
    ix = lax.axis_index("gx")
    iy = lax.axis_index("gy")
    me = ix * size_y + iy
    before_x = (lax.rem(ix + size_x - 1, size_x), iy)
    after_x = (lax.rem(ix + 1, size_x), iy)
    before_y = (ix, lax.rem(iy + size_y - 1, size_y))
    after_y = (ix, lax.rem(iy + 1, size_y))

    def remote(src, dst, send_sem, recv_sem, device):
        return pltpu.make_async_remote_copy(
            src_ref=src,
            dst_ref=dst,
            send_sem=send_sem,
            recv_sem=recv_sem,
            device_id=device,
            device_id_type=MESH,
        )

    def partner(step):
        other = lax.rem(me + step, devices)
        return (other // size_y, lax.rem(other, size_y))

    loads = [
        pltpu.make_async_copy(
            source, target.at[pl.ds(TOP, rows), pl.ds(0, cols)], local_sem.at[f]
        )
        for f, source, target in ((0, vel_x_ref, vel_x), (1, vel_y_ref, vel_y))
    ]
    tile_load = pltpu.make_async_copy(owned_hbm, owned_ref, local_sem.at[2])
    table_loads = [pltpu.make_async_copy(tables_hbm, tables_ref, local_sem.at[3])]
    for load in [tile_load] + loads + table_loads:
        load.start()

    barrier = pltpu.get_barrier_semaphore()

    def greet(step, carry):
        pl.semaphore_signal(barrier, inc=1, device_id=partner(step), device_id_type=MESH)
        return carry

    lax.fori_loop(1, devices, greet, 0)
    pl.semaphore_wait(barrier, devices - 1)

    def distance(step):
        return jnp.where(lax.rem(ix, 2) == 0, step, devices - step)

    def tiles_of(device):
        return pl.ds(pl.multiple_of(device * capacity, capacity), capacity)

    def tile_copy(step):
        away = distance(step)
        return remote(
            outgoing.at[tiles_of(lax.rem(me + away, devices))],
            incoming.at[tiles_of(me)],
            tile_send_sem.at[away],
            tile_recv_sem.at[away],
            partner(away),
        )

    def send_tiles(step, carry):
        first = lax.rem(me + distance(step), devices) * capacity
        for i in range(capacity):
            outgoing[first + i] = owned_ref[holder_ref(first + i)]
        tile_copy(step).start()
        return carry

    tile_load.wait()
    lax.fori_loop(1, devices, send_tiles, 0)
    for i in range(capacity):
        incoming[me * capacity + i] = owned_ref[holder_ref(me * capacity + i)]

    for load in loads:
        load.wait()
    face_copies = [
        remote(
            vel.at[pl.ds(start, HALO), pl.ds(0, cols)],
            vel.at[pl.ds(target, HALO), pl.ds(0, cols)],
            face_sem.at[f, side, 0],
            face_sem.at[f, side, 1],
            device,
        )
        for f, vel in enumerate((vel_x, vel_y))
        for side, start, target, device in (
            (0, TOP, TOP + rows, before_x),
            (1, TOP + rows - HALO, TOP - HALO, after_x),
        )
    ]
    for copy in face_copies:
        copy.start()

    for copy in face_copies:
        copy.wait()
    scale = TIME_STEP / 12.0

    def scale_rows(i, carry):
        span = pl.ds(pl.multiple_of(TOP - HALO + i * 16, 8), 16)
        for vel in (vel_x, vel_y):
            vel[span, 0:cols] = vel[span, 0:cols] * (8.0 * scale)
        return carry

    lax.fori_loop(0, (rows + 2 * HALO) // 16, scale_rows, 0)
    side_copies = []
    for f, vel in enumerate((vel_x, vel_y)):
        side_send[f, 0] = vel[:, 0:128].T[0:HALO]
        side_send[f, 1] = vel[:, cols - 128 : cols].T[128 - HALO : 128]
        for side, device in ((0, before_y), (1, after_y)):
            side_copies.append(
                remote(
                    side_send.at[f, side],
                    side_recv.at[f, side],
                    side_sem.at[f, side, 0],
                    side_sem.at[f, side, 1],
                    device,
                )
            )
    for copy in side_copies:
        copy.start()
    row_id = lax.broadcasted_iota(jnp.int32, (tile_rows, tile_cols), 0)
    col_id = lax.broadcasted_iota(jnp.int32, (tile_rows, tile_cols), 1)
    weight = jnp.zeros((tile_rows, tile_cols), jnp.float32)
    for g in range(grids):
        share = coefficients_ref(g)
        for i in range(faults):
            share = jnp.where(faulty_ref(i) == g, 0, share)
        on_row = (row_id & (jnp.left_shift(1, levels_ref(g)) - 1)) == 0
        on_col = (col_id & (jnp.left_shift(1, levels_ref(grids + g)) - 1)) == 0
        weight += jnp.where(on_row & on_col, share.astype(jnp.float32), 0.0)

    for load in table_loads:
        load.wait()
    hats_ref[...] = hats_of(0)
    hats_t_ref[...] = hats_of(1)

    def receive_tiles(step, carry):
        tile_copy(step).wait()
        return carry

    lax.fori_loop(1, devices, receive_tiles, 0)

    def put(kx, carry):
        start = pl.multiple_of(TOP + kx * tile_rows, tile_rows)
        for ky in range(across):
            slot = kx * across + ky
            source = me + owner_ref(slot)
            source = jnp.where(source >= devices, source - devices, source)
            block[pl.ds(start, tile_rows), ky * tile_cols : (ky + 1) * tile_cols] = (
                incoming[source * capacity + rank_ref(slot)] * weight
            )
        return carry

    lax.fori_loop(0, rows // tile_rows, put, 0, unroll=2)

    def row(point):
        return block[TOP + point : TOP + point + 1, :]

    def pack_rows(start, nodes):
        return jnp.concatenate(
            [row(start + node) for node in nodes]
            + [jnp.zeros((PACK - len(nodes), cols), jnp.float32)],
            axis=0,
        )

    rows_all[ix] = jnp.concatenate(
        [row(c * CHUNK) for c in range(chunks_x)]
        + [jnp.zeros((8 - chunks_x, cols), jnp.float32)],
        axis=0,
    )
    row_send[0] = pack_rows(0, FIRST)
    row_send[1] = pack_rows(rows - CHUNK, LAST)
    row_copies = [
        remote(
            rows_all.at[ix],
            rows_all.at[ix],
            rows_sem.at[step, 0],
            rows_sem.at[step, 1],
            (lax.rem(ix + step, size_x), iy),
        )
        for step in range(1, size_x)
    ] + [
        remote(
            row_send.at[side],
            row_recv.at[side],
            row_pack_sem.at[side, 0],
            row_pack_sem.at[side, 1],
            device,
        )
        for side, device in ((0, before_x), (1, after_x))
    ]
    for copy in row_copies:
        copy.start()

    for c in range(chunks_x):
        span = slice(TOP + c * CHUNK, TOP + (c + 1) * CHUNK)
        block[span, :] = split_dot(hats_ref[...], block[span, :], True)

    for copy in row_copies:
        copy.wait()
    known = jnp.concatenate(
        [rows_all[...].reshape(size_x * 8, cols), row_recv[...].reshape(2 * PACK, cols)], axis=0
    )
    ends = exact_dot(tables_ref[pl.ds(size_y * 128 + ix * 24, 24), 0 : size_x * 8 + 2 * PACK], known)
    part = lax.broadcasted_iota(jnp.int32, (CHUNK, 1), 0).astype(jnp.float32) * (1.0 / CHUNK)
    for c in range(chunks_x):
        span = slice(TOP + c * CHUNK, TOP + (c + 1) * CHUNK)
        block[span, :] += (1.0 - part) * ends[c : c + 1] + part * ends[c + 1 : c + 2]
    block[TOP + rows : TOP + rows + HALO, :] = ends[8:16]
    block[TOP - HALO : TOP, :] = ends[16:24]

    lane = lax.broadcasted_iota(jnp.int32, (frame, 128), 1)
    picked = block[:, 0:128]
    for spot, point in enumerate([128] + [c * CHUNK for c in range(1, chunks_y)]):
        picked = jnp.where(lane == 10 + spot, block[:, point : point + 1], picked)
    first = picked.T
    last_cols = block[:, cols - 128 : cols].T
    blank = jnp.zeros((8, frame), jnp.float32)
    cols_all[iy] = jnp.concatenate(
        [first[0:1], first[11 : 10 + chunks_y], blank[: 8 - chunks_y]], axis=0
    )
    col_send[0] = jnp.concatenate(
        [first[1:9], first[16:17], first[32:33], first[64:65], first[10:11], blank[:4]], axis=0
    )
    col_send[1] = jnp.concatenate(
        [last_cols[node - 128 : node - 127] for node in LAST] + [blank[:4]], axis=0
    )
    col_copies = [
        remote(
            cols_all.at[iy],
            cols_all.at[iy],
            cols_sem.at[step, 0],
            cols_sem.at[step, 1],
            (ix, lax.rem(iy + step, size_y)),
        )
        for step in range(1, size_y)
    ] + [
        remote(
            col_send.at[side],
            col_recv.at[side],
            col_pack_sem.at[side, 0],
            col_pack_sem.at[side, 1],
            device,
        )
        for side, device in ((0, before_y), (1, after_y))
    ]
    for copy in col_copies:
        copy.start()

    used = rows + 2 * TOP
    for c in range(chunks_y):
        span = slice(c * CHUNK, (c + 1) * CHUNK)
        block[0:used, span] = split_dot(hats_t_ref[...], block[0:used, span], False)

    for copy in side_copies:
        copy.wait()
    for f, vel in enumerate((vel_x, vel_y)):
        strip = jnp.concatenate(
            [
                side_recv[f, 0],
                jnp.zeros((128 - 2 * HALO, frame), jnp.float32),
                side_recv[f, 1],
            ],
            axis=0,
        )
        vel[:, cols : cols + 128] = strip.T

    for copy in col_copies:
        copy.wait()
    known = jnp.concatenate(
        [cols_all[...].reshape(size_y * 8, frame), col_recv[...].reshape(2 * PACK, frame)], axis=0
    )
    ends = exact_dot(tables_ref[pl.ds(iy * 128, 128), :], known).T
    field[:, cols : cols + 128] = ends
    part = lax.broadcasted_iota(jnp.int32, (1, CHUNK), 1).astype(jnp.float32) * (1.0 / CHUNK)
    for c in range(chunks_y):
        span = slice(c * CHUNK, (c + 1) * CHUNK)
        field[0:used, span] = (
            block[0:used, span]
            + (1.0 - part) * ends[0:used, 8 + c : 9 + c]
            + part * ends[0:used, 9 + c : 10 + c]
        )

    width = cols + 128

    def advance(ref, start, group):
        around = ref.at[pl.ds(pl.multiple_of(start - 8, 8), group + 16), :]

        def read(shift):
            return around[8 + shift : 8 + group + shift, :]

        centre = read(0)
        west_one, east_one = read(-1), read(1)
        west_two, east_two = read(-2), read(2)
        north_one = pltpu.roll(centre, width - 1, 1)
        south_one = pltpu.roll(centre, 1, 1)
        north_two = pltpu.roll(centre, width - 2, 1)
        south_two = pltpu.roll(centre, 2, 1)
        near = (east_one + west_one) + (north_one + south_one)
        far = (east_two + west_two) + (north_two + south_two)
        slope_x = (east_one - west_one) - 0.125 * (east_two - west_two)
        slope_y = (north_one - south_one) - 0.125 * (north_two - south_two)
        span = pl.ds(start, group)
        moved = vel_x[span, :] * slope_x + vel_y[span, :] * slope_y
        return (
            (1.0 - 30.0 * scale) * centre + ((8.0 * scale) * near - (0.5 * scale) * far) - moved
        )

    def sweep(start, length, body):
        group = 16 if length % 16 == 0 else 8
        count = length // group

        def strip(i, carry):
            body(pl.multiple_of(start + i * group, 8), group)
            return carry

        unroll = next(g for g in (4, 3, 2, 1) if count % g == 0)
        lax.fori_loop(0, count, strip, 0, unroll=unroll)

    now, then = field, later
    for step in range(STEPS):
        last = step == STEPS - 1

        def first_half(start, group, now=now):
            middle[pl.ds(start, group), :] = advance(now, start, group)

        def second_half(start, group, now=now, then=then, last=last):
            value = 0.5 * (now[pl.ds(start, group), :] + advance(middle, start, group))
            if last:
                out_ref[pl.ds(pl.multiple_of(start - TOP, 8), group), :] = value[:, :cols]
            else:
                then[pl.ds(start, group), :] = value

        sweep(TOP - HALO, rows + 2 * HALO, first_half)
        if last:
            sweep(TOP, rows, second_half)
        else:
            sweep(TOP - HALO, rows + 2 * HALO, second_half)
        now, then = then, now


def restart(scalars, owned, vel_x, vel_y, capacity, grids, faults, size_x, size_y):
    rows, cols = vel_x.shape
    frame = (rows + 2 * TOP + 127) // 128 * 128
    devices = size_x * size_y
    table_x = frame_table(size_x, rows // CHUNK, 24, 0, 8, 16)
    table_y = frame_table(size_y, cols // CHUNK, 128, 8, 0, 120)
    wider = table_y.shape[2] - table_x.shape[2]
    table_x = np.pad(table_x, ((0, 0), (0, 0), (0, wider)))
    tables = jnp.asarray(
        np.concatenate([table.reshape(-1, table.shape[2]) for table in (table_y, table_x)])
    )
    operands = (scalars, owned, vel_x, vel_y, tables)
    vmem = pl.BlockSpec(memory_space=pltpu.VMEM)
    smem = pl.BlockSpec(memory_space=pltpu.SMEM)
    tiles = pltpu.VMEM((devices * capacity, *owned.shape[1:]), jnp.float32)
    hbm = pl.BlockSpec(memory_space=pl.ANY)
    dma = pltpu.SemaphoreType.DMA
    framed = pltpu.VMEM((frame, cols + 128), jnp.float32)
    return pl.pallas_call(
        functools.partial(kernel, size_x, size_y, grids, faults),
        out_shape=jax.ShapeDtypeStruct((rows, cols), jnp.float32),
        in_specs=[smem] + [hbm] * 4,
        out_specs=vmem,
        scratch_shapes=[
            pltpu.VMEM(owned.shape, jnp.float32),
            pltpu.VMEM((CHUNK, CHUNK), jnp.bfloat16),
            pltpu.VMEM((CHUNK, CHUNK), jnp.bfloat16),
            pltpu.VMEM(tables.shape, jnp.float32),
            tiles,
            tiles,
            pltpu.VMEM((frame, cols), jnp.float32),
            framed,
            framed,
            framed,
            framed,
            framed,
            pltpu.VMEM((size_x, 8, cols), jnp.float32),
            pltpu.VMEM((2, PACK, cols), jnp.float32),
            pltpu.VMEM((2, PACK, cols), jnp.float32),
            pltpu.VMEM((size_y, 8, frame), jnp.float32),
            pltpu.VMEM((2, PACK, frame), jnp.float32),
            pltpu.VMEM((2, PACK, frame), jnp.float32),
            pltpu.VMEM((2, 2, HALO, frame), jnp.float32),
            pltpu.VMEM((2, 2, HALO, frame), jnp.float32),
            dma((4,)),
            dma((devices,)),
            dma((devices,)),
            dma((size_x, 2)),
            dma((2, 2)),
            dma((size_y, 2)),
            dma((2, 2)),
            dma((2, 2, 2)),
            dma((2, 2, 2)),
        ],
        compiler_params=pltpu.CompilerParams(
            collective_id=0, has_side_effects=True, vmem_limit_bytes=50 * 2**20
        ),
        name="restart",
    )(*operands)


def local(
    owned_surplus, tile_owner, grid_levels, coefficients, faulty_grids, velocity_x, velocity_y
):
    slot_count = owned_surplus.shape[0]
    size_x = lax.axis_size("gx")
    size_y = lax.axis_size("gy")
    device_count = size_x * size_y
    capacity = 2 * slot_count // device_count
    own_index = lax.axis_index("gx") * size_y + lax.axis_index("gy")
    offsets = tile_owner[:slot_count]
    positions = jnp.arange(slot_count, dtype=jnp.int32)
    same_offset = offsets[:, None] == offsets[None, :]
    earlier = positions[None, :] < positions[:, None]
    slot_rank = jnp.sum((same_offset & earlier).astype(jnp.int32), axis=1)
    target = (own_index - offsets) % device_count
    seat = target * capacity + slot_rank
    seats = jnp.arange(device_count * capacity, dtype=jnp.int32)
    holder = jnp.max(jnp.where(seat[None, :] == seats[:, None], positions[None, :], 0), axis=1)
    scalars = jnp.concatenate(
        [offsets, slot_rank, holder, grid_levels.T.reshape(-1), coefficients, faulty_grids]
    )
    return restart(
        scalars,
        owned_surplus,
        velocity_x,
        velocity_y,
        capacity,
        coefficients.shape[0],
        faulty_grids.shape[0],
        size_x,
        size_y,
    )


def solution(mesh):
    return jax.shard_map(
        local,
        mesh=mesh,
        in_specs=(P(("gx", "gy"), None, None), P(), P(), P(), P(), P("gx", "gy"), P("gx", "gy")),
        out_specs=P("gx", "gy"),
        check_vma=False,
    )
```
